128 devices in a mesh: stretch: 16 (over z, x_lo, core), grp: 8 (over x_hi, y).
Axes of the slice: x: 4 (x_hi: 2, x_lo: 2; x = x_hi * 2 + x_lo), y: 4, z: 4, core: 2. Of those that a mesh axis runs over, the one named last changes fastest.
Arguments:
- queries: bfloat16 [16384, 4096], P(('stretch', 'grp')), may hold values from -6 to 6
- keys: bfloat16 [16384, 4096], P(('stretch', 'grp')), may hold values from -6 to 6
- values: bfloat16 [16384, 4096], P(('stretch', 'grp')), may hold values from -6 to 6
- short_filter: float32 [3, 3, 4096], replicated, may hold values from -3 to 3
- long_filter: bfloat16 [3072, 4096], P(None, 'grp'), may hold values from -0.109375 to 0.109375
- skip_gain: float32 [4096], P('grp'), may hold values from -4 to 4
Outputs:
- filtered: bfloat16 [16384, 4096], P('stretch', 'grp')
The draws below stay inside these ranges and needn't reach their ends.
All inputs are finite; a program needn't handle non-finite values.
Results may differ from the reference program's by a relative error of at most 0.012.
Values may be sent and summed in bfloat16 or wider, within the bound.
A program may use at most 128 MiB of HBM per device.

```python
import jax
import jax.numpy as jnp
from jax import lax

D = 4096
FILTER_LEN = 3072
TOKENS = 16384


def block_levels(own_key, extent, shards, least, high):
    loudness, own = 1.0, jax.random.fold_in(own_key, 6)
    for axis_at, blocks in shards:
        draws = jnp.exp(jax.random.uniform(jax.random.fold_in(own, axis_at), (blocks,), jnp.float32, least / len(shards), high / len(shards)))
        loudness = loudness * jnp.repeat(draws, extent[axis_at] // blocks).reshape([-1 if axis == axis_at else 1 for axis in range(len(extent))])
    return loudness


def centred(own_key, extent, scale, most, split=(), dtype=jnp.bfloat16):
    level = block_levels(own_key, extent, split, -0.22, 0.18) if split else 1.0
    entries = jax.random.normal(own_key, extent, jnp.float32) * scale * level
    return jnp.minimum(jnp.maximum(entries, -most), most).astype(dtype)


def setup_inputs(seed: int = 0) -> dict:
    streams_of = jax.random.split(jax.random.key(seed), 7)
    return {
        "queries": centred(streams_of[0], (TOKENS, D), 1.0, 6.0, ((0, 128),)),
        "keys": centred(streams_of[1], (TOKENS, D), 1.0, 6.0, ((0, 128),)),
        "values": centred(streams_of[2], (TOKENS, D), 1.0, 6.0, ((0, 128),)),
        "short_filter": centred(streams_of[3], (3, 3, D), 0.5, 3.0, (), jnp.float32),
        "long_filter": centred(streams_of[4], (FILTER_LEN, D), FILTER_LEN ** -0.5, 0.109375, ((1, 8),)),
        "skip_gain": centred(streams_of[5], (D,), 1.0, 4.0, ((0, 8),), jnp.float32),
    }


def shorten(signal, short_filter, position):
    padded = jnp.pad(signal.astype(jnp.float32), ((2, 0), (0, 0)))
    return short_filter[0, position] * padded[2:] + short_filter[1, position] * padded[1:-1] + short_filter[2, position] * padded[:-2]


def convolve(operands):
    signal, filters = operands
    padded_len = TOKENS + FILTER_LEN
    product = jnp.fft.rfft(signal, n=padded_len, axis=0) * jnp.fft.rfft(filters, n=padded_len, axis=0)
    return jnp.fft.irfft(product, n=padded_len, axis=0)[:TOKENS]


def reference(queries, keys, values, short_filter, long_filter, skip_gain):
    q_short = shorten(queries, short_filter, 0).astype(jnp.bfloat16)
    gated = (shorten(keys, short_filter, 1) * shorten(values, short_filter, 2)).astype(jnp.bfloat16)
    group_width = min(256, D)
    groups = D // group_width
    signal = gated.astype(jnp.float32).reshape(TOKENS, groups, group_width).transpose(1, 0, 2)
    filters = long_filter.astype(jnp.float32).reshape(FILTER_LEN, groups, group_width).transpose(1, 0, 2)
    convolved = lax.map(convolve, (signal, filters)).transpose(1, 0, 2).reshape(TOKENS, D)
    result = q_short.astype(jnp.float32) * (convolved + skip_gain * gated.astype(jnp.float32))
    return result.astype(jnp.bfloat16)
```

```python
import jax
import jax.numpy as jnp
import ml_dtypes
import numpy as np
from jax import lax
from jax.experimental import pallas as pl
from jax.experimental.pallas import tpu as pltpu
from jax.sharding import PartitionSpec as P

MESH = pl.DeviceIdType.MESH
BLOCK = 512
LANES = 128
ROWS = 128
PIECES = 4
GROUPS = 8
PEERS = PIECES * GROUPS
PIECE = ROWS * GROUPS
TAPS = 3072
HALO = TAPS // BLOCK
OWN = PIECES * PIECE // BLOCK
BF16, F32 = jnp.bfloat16, jnp.float32


def tables():
    n, m = np.arange(BLOCK), np.arange(BLOCK)
    phase = ((4 * m[:, None] + 1) * n[None, :]) % (4 * BLOCK)
    angle = 2.0 * np.pi * phase / (4 * BLOCK)
    forward = np.concatenate([np.cos(angle), -np.sin(angle)], axis=0)

    def parts(table):
        high = table.astype(ml_dtypes.bfloat16)
        return high, (table - high.astype(np.float64)).astype(ml_dtypes.bfloat16)

    high, low = parts(forward)
    back_high, back_low = parts(forward.T / BLOCK)
    return np.concatenate([high, low], axis=1), np.stack([back_high, back_low])


def kernel(
    queries,
    keys,
    values,
    short_filter,
    long_filter,
    skip_gain,
    forward_hbm,
    inverse_hbm,
    q_out,
    r_out,
    key_buf,
    value_buf,
    query_buf,
    short_buf,
    filter_buf,
    forward,
    inverse,
    edge_out,
    edge_in,
    edge,
    gated_buf,
    q_buf,
    signal,
    spectra,
    filter_spectra,
    product,
    result,
    load_sem,
    edge_sem,
    gated_send,
    gated_recv,
    halo_send,
    halo_recv,
    q_send,
    q_recv,
    r_send,
    r_recv,
    own_sem,
):
    stretch, grp = lax.axis_index("stretch"), lax.axis_index("grp")
    plane, piece = lax.div(stretch, PIECES), lax.rem(stretch, PIECES)
    half, row = lax.div(grp, 4), lax.rem(grp, 4)

    def peer(step, sign):
        kp, ky, kx = lax.rem(step, 4), lax.rem(lax.div(step, 4), 4), lax.div(step, 16)
        p = lax.rem(piece + sign * kp + 4, 4)
        y = lax.rem(row + sign * ky + 4, 4)
        h = lax.rem(half + kx, 2)
        return p, h * 4 + y

    def place(p, g):
        return HALO + 2 * p + lax.div(g, 4), pl.ds(pl.multiple_of(lax.rem(g, 4) * ROWS, ROWS), ROWS)

    own_lanes = pl.ds(pl.multiple_of(piece * LANES, LANES), LANES)
    loads = [
        pltpu.make_async_copy(keys, key_buf, load_sem.at[0]),
        pltpu.make_async_copy(values, value_buf, load_sem.at[1]),
        pltpu.make_async_copy(queries, query_buf, load_sem.at[2]),
        pltpu.make_async_copy(short_filter, short_buf, load_sem.at[3]),
        pltpu.make_async_copy(long_filter.at[:, :, own_lanes], filter_buf, load_sem.at[4]),
        pltpu.make_async_copy(forward_hbm, forward, load_sem.at[5]),
        pltpu.make_async_copy(inverse_hbm, inverse, load_sem.at[6]),
    ]
    for load in loads:
        load.start()

    barrier = pltpu.get_barrier_semaphore()

    def greet(step, carry):
        p, g = peer(step, 1)
        pl.semaphore_signal(barrier, inc=1, device_id=(plane * PIECES + p, g), device_id_type=MESH)
        return carry

    lax.fori_loop(1, PEERS, greet, 0)
    has_before, has_after = plane > 0, plane < 3
    corner = jnp.logical_and(piece == PIECES - 1, grp == GROUPS - 1)

    @pl.when(has_before)
    def _():
        pl.semaphore_signal(barrier, inc=1, device_id=(stretch - PIECES, grp), device_id_type=MESH)

    @pl.when(jnp.logical_and(has_before, jnp.logical_and(piece == 0, grp == 0)))
    def _():
        pl.semaphore_signal(barrier, inc=1, device_id=(stretch - 1, GROUPS - 1), device_id_type=MESH)

    @pl.when(jnp.logical_not(has_before))
    def _():
        signal[:HALO] = jnp.zeros((HALO, BLOCK, LANES), BF16)

    for load in loads[:4]:
        load.wait()
    fold = 512
    row_at = lax.broadcasted_iota(jnp.int32, (16, fold), 0)
    for n, buf in enumerate((key_buf, value_buf, query_buf)):
        tail = buf[ROWS - 16 :, :].astype(F32)
        packed = jnp.zeros((16, fold), F32)
        for r in range(2):
            for e in range(8):
                part = tail[14 + r : 15 + r, e * fold : (e + 1) * fold]
                packed = jnp.where(row_at == r * 8 + e, part, packed)
        edge_out[n] = packed.astype(BF16)

    after = has_after.astype(jnp.int32)
    pl.semaphore_wait(barrier, PEERS - 1 + after + after * corner.astype(jnp.int32))

    wraps = grp == GROUPS - 1
    next_device = (
        jnp.where(wraps, lax.rem(stretch + 1, 16), stretch),
        jnp.where(wraps, 0, grp + 1),
    )
    edge_copy = pltpu.make_async_remote_copy(
        edge_out, edge_in, edge_sem.at[0], edge_sem.at[1], device_id=next_device, device_id_type=MESH
    )
    is_first = jnp.logical_and(stretch == 0, grp == 0)
    is_last = jnp.logical_and(stretch == 15, wraps)

    @pl.when(jnp.logical_not(is_last))
    def _():
        edge_copy.start()

    @pl.when(is_first)
    def _():
        edge_in[...] = jnp.zeros_like(edge_in)

    @pl.when(jnp.logical_not(is_first))
    def _():
        edge_copy.wait_recv()

    for n in range(3):
        packed = edge_in[n].astype(F32)
        for r in range(2):
            for e in range(8):
                edge[n, r : r + 1, e * fold : (e + 1) * fold] = packed[r * 8 + e : r * 8 + e + 1]

    at = lax.broadcasted_iota(jnp.int32, (ROWS, LANES), 0)

    def shorten(buf, n, position, block):
        lanes = pl.ds(pl.multiple_of(block * LANES, LANES), LANES)
        now = buf[:, lanes].astype(F32)
        two, one = edge[n, 0:1, lanes], edge[n, 1:2, lanes]
        back1 = jnp.where(at == 0, one, pltpu.roll(now, 1, 0))
        back2 = jnp.where(at == 0, two, jnp.where(at == 1, one, pltpu.roll(now, 2, 0)))
        taps = [short_buf[tap, position : position + 1, lanes] for tap in range(3)]
        return taps[0] * now + taps[1] * back1 + taps[2] * back2

    def gated_copy(step):
        p, g = peer(step, 1)
        block, rows = place(piece, grp)
        return pltpu.make_async_remote_copy(
            gated_buf.at[step],
            signal.at[block, rows],
            gated_send.at[step],
            gated_recv.at[step],
            device_id=(plane * PIECES + p, g),
            device_id_type=MESH,
        )

    def make_gated(step):
        p, g = peer(step, 1)
        block = g * PIECES + p
        gated_buf[step] = (shorten(key_buf, 0, 1, block) * shorten(value_buf, 1, 2, block)).astype(BF16)

    def send_gated(step, carry):
        make_gated(step)
        gated_copy(step).start()
        return carry

    lax.fori_loop(1, PEERS, send_gated, 0)
    make_gated(0)
    own_block, own_rows = place(piece, grp)
    own_gated = pltpu.make_async_copy(gated_buf.at[0], signal.at[own_block, own_rows], gated_recv.at[0])
    own_gated.start()

    def halo_copy(step):
        p, g = peer(step, -1)
        block, rows = place(p, g)
        return pltpu.make_async_remote_copy(
            signal.at[block, rows],
            signal.at[block - OWN, rows],
            halo_send.at[step],
            halo_recv.at[p],
            device_id=(lax.rem(stretch + PIECES, 16), grp),
            device_id_type=MESH,
        )

    def pass_on(step):
        p, _ = peer(step, -1)

        @pl.when(jnp.logical_and(has_after, p > 0))
        def _():
            halo_copy(step).start()

    def transform(source, block, target, rows):
        pair = jnp.concatenate([source[block], source[block + 1]], axis=1)
        bins = jnp.dot(forward[rows, :], jnp.concatenate([pair, pair], axis=0), preferred_element_type=F32)
        target[block, rows] = bins[:, :LANES]
        target[block + 1, rows] = bins[:, LANES:]

    def shorten_q(block):
        lanes = pl.ds(pl.multiple_of(block * LANES, LANES), LANES)
        q_buf[:, lanes] = shorten(query_buf, 2, 0, block).astype(BF16)

    own_gated.wait()
    pass_on(0)
    shorten_q(0)
    for load in loads[4:]:
        load.wait()

    def receive(step, carry):
        shorten_q(step)

        @pl.when(lax.rem(step, 5) == 0)
        def _():
            unit = lax.div(step, 5) - 1
            half_rows = pl.ds(pl.multiple_of(lax.rem(unit, 2) * BLOCK, BLOCK), BLOCK)
            transform(filter_buf, 2 * lax.div(unit, 2), filter_spectra, half_rows)

        gated_copy(step).wait_recv()
        pass_on(step)
        return carry

    lax.fori_loop(1, PEERS, receive, 0)

    def q_copy(step):
        other = lax.rem(grp + step, GROUPS)
        return pltpu.make_async_remote_copy(
            q_buf.at[:, pl.ds(pl.multiple_of(other * 512, 512), 512)],
            q_out.at[pl.ds(pl.multiple_of(grp * ROWS, ROWS), ROWS)],
            q_send.at[step],
            q_recv.at[step],
            device_id=(stretch, other),
            device_id_type=MESH,
        )

    own_q = pltpu.make_async_copy(
        q_buf.at[:, pl.ds(pl.multiple_of(grp * 512, 512), 512)],
        q_out.at[pl.ds(pl.multiple_of(grp * ROWS, ROWS), ROWS)],
        own_sem.at[0],
    )
    own_q.start()
    for step in range(1, GROUPS):
        q_copy(step).start()

    def transform_signal(first, count):
        def body(unit, carry):
            half_rows = pl.ds(pl.multiple_of(lax.rem(unit, 2) * BLOCK, BLOCK), BLOCK)
            transform(signal, first + 2 * lax.div(unit, 2), spectra, half_rows)
            return carry

        lax.fori_loop(0, count, body, 0)

    gain = skip_gain[own_lanes].reshape(1, LANES)

    def convolve(p):
        def bins(tile, carry):
            real = pl.ds(pl.multiple_of(tile * 16, 16), 16)
            imag = pl.ds(pl.multiple_of(BLOCK + tile * 16, 16), 16)
            window = []
            for b in range(HALO + 1):
                here, before = 2 * p + 1 + b, 2 * p + b
                window.append(
                    (
                        spectra[here, real] - spectra[before, imag],
                        spectra[here, imag] + spectra[before, real],
                    )
                )
            sums = [None, None]
            for i in range(HALO):
                fr, fi = filter_spectra[i, real], filter_spectra[i, imag]
                for o in range(2):
                    sr, si = window[HALO - 1 + o - i]
                    re, im = fr * sr - fi * si, fr * si + fi * sr
                    sums[o] = (re, im) if sums[o] is None else (sums[o][0] + re, sums[o][1] + im)
            for at_rows, n in ((real, 0), (imag, 1)):
                both = jnp.concatenate([sums[0][n], sums[1][n]], axis=1)
                high = both.astype(BF16)
                product[0, at_rows] = high
                product[1, at_rows] = (both - high.astype(F32)).astype(BF16)
            return carry

        lax.fori_loop(0, BLOCK // 16, bins, 0)
        back = (
            jnp.dot(inverse[0], product[0], preferred_element_type=F32)
            + jnp.dot(inverse[0], product[1], preferred_element_type=F32)
            + jnp.dot(inverse[1], product[0], preferred_element_type=F32)
        )
        for o in range(2):
            direct = gain * signal[HALO + 2 * p + o].astype(F32)
            result[p, pl.ds(o * BLOCK, BLOCK)] = (back[:, o * LANES : (o + 1) * LANES] + direct).astype(BF16)

    def r_copy(p):
        return pltpu.make_async_remote_copy(
            result.at[p],
            r_out.at[:, own_lanes],
            r_send.at[p],
            r_recv.at[piece],
            device_id=(plane * PIECES + p, grp),
            device_id_type=MESH,
        )

    own_r = pltpu.make_async_copy(result.at[piece], r_out.at[:, own_lanes], own_sem.at[1])

    def send_result(p):
        @pl.when(piece != p)
        def _():
            r_copy(p).start()

        @pl.when(piece == p)
        def _():
            own_r.start()

    transform_signal(HALO, 2 * PIECES)
    convolve(3)
    send_result(3)
    for p in (2, 1, 0):

        @pl.when(has_before)
        def _(p=p):
            blocks = signal.at[pl.ds(2 * p, 2)]
            pltpu.make_async_copy(blocks, blocks, halo_recv.at[p + 1]).wait()

        transform_signal(2 * p, 2)
        convolve(p)
        send_result(p)

    own_q.wait()
    for step in range(1, GROUPS):
        q_copy(step).wait()
    own_r.wait()
    for p in range(PIECES):

        @pl.when(piece != p)
        def _(p=p):
            r_copy(p).wait_send()
            lanes = pl.ds(p * LANES, LANES)
            pltpu.make_async_copy(r_out.at[:, lanes], r_out.at[:, lanes], r_recv.at[p]).wait()

    @pl.when(jnp.logical_not(is_last))
    def _():
        edge_copy.wait_send()

    def sent(step, carry):
        gated_copy(step).wait_send()
        return carry

    lax.fori_loop(1, PEERS, sent, 0)

    def halo_sent(step, carry):
        p, _ = peer(step, -1)

        @pl.when(jnp.logical_and(has_after, p > 0))
        def _():
            halo_copy(step).wait_send()

        return carry

    lax.fori_loop(0, PEERS, halo_sent, 0)


def local(queries, keys, values, short_filter, long_filter, skip_gain):
    width = queries.shape[1]
    slice_width = width // GROUPS
    forward, inverse = tables()
    hbm, vmem = pl.BlockSpec(memory_space=pl.ANY), pl.BlockSpec(memory_space=pltpu.VMEM)
    dma = pltpu.SemaphoreType.DMA
    q_slices, convolved = pl.pallas_call(
        kernel,
        out_shape=[jax.ShapeDtypeStruct((PIECE, slice_width), BF16)] * 2,
        in_specs=[hbm, hbm, hbm, hbm, hbm, vmem, hbm, hbm],
        out_specs=[hbm, hbm],
        scratch_shapes=[
            pltpu.VMEM((ROWS, width), BF16),
            pltpu.VMEM((ROWS, width), BF16),
            pltpu.VMEM((ROWS, width), BF16),
            pltpu.VMEM((3, 3, width), F32),
            pltpu.VMEM((HALO, BLOCK, LANES), BF16),
            pltpu.VMEM(forward.shape, BF16),
            pltpu.VMEM(inverse.shape, BF16),
            pltpu.VMEM((3, 16, 512), BF16),
            pltpu.VMEM((3, 16, 512), BF16),
            pltpu.VMEM((3, 8, width), F32),
            pltpu.VMEM((PEERS, ROWS, LANES), BF16),
            pltpu.VMEM((ROWS, width), BF16),
            pltpu.VMEM((HALO + OWN, BLOCK, LANES), BF16),
            pltpu.VMEM((HALO + OWN, 2 * BLOCK, LANES), F32),
            pltpu.VMEM((HALO, 2 * BLOCK, LANES), F32),
            pltpu.VMEM((2, 2 * BLOCK, 2 * LANES), BF16),
            pltpu.VMEM((PIECES, PIECE, LANES), BF16),
            dma((7,)),
            dma((2,)),
            dma((PEERS,)),
            dma((PEERS,)),
            dma((PEERS,)),
            dma((PIECES,)),
            dma((GROUPS,)),
            dma((GROUPS,)),
            dma((PIECES,)),
            dma((PIECES,)),
            dma((2,)),
        ],
        compiler_params=pltpu.CompilerParams(
            collective_id=0, has_side_effects=True, vmem_limit_bytes=56 * 2**20
        ),
        cost_estimate=pl.CostEstimate(flops=9 * 10**9, bytes_accessed=16 * 2**20, transcendentals=0),
    )(
        queries,
        keys,
        values,
        short_filter,
        long_filter.reshape(HALO, BLOCK, slice_width),
        skip_gain,
        jnp.asarray(forward),
        jnp.asarray(inverse),
    )
    return (q_slices.astype(F32) * convolved.astype(F32)).astype(BF16)


def solution(mesh):
    return jax.shard_map(
        local,
        mesh=mesh,
        in_specs=(
            P(("stretch", "grp"), None),
            P(("stretch", "grp"), None),
            P(("stretch", "grp"), None),
            P(),
            P(None, "grp"),
            P("grp"),
        ),
        out_specs=P("stretch", "grp"),
        check_vma=False,
    )
```

```python
import jax
import jax.numpy as jnp
import ml_dtypes
import numpy as np
from jax import lax
from jax.experimental import pallas as pl
from jax.experimental.pallas import tpu as pltpu
from jax.sharding import PartitionSpec as P

MESH = pl.DeviceIdType.MESH
BLOCK = 512
LANES = 128
ROWS = 128
HEAD = 16
PIECES = 4
GROUPS = 8
PEERS = PIECES * GROUPS
PIECE = ROWS * GROUPS
TAPS = 3072
HALO = TAPS // BLOCK
OWN = PIECES * PIECE // BLOCK
HALO_PIECES = TAPS // PIECE
AHEAD = 16
PROMPT = 2
BF16, F32 = jnp.bfloat16, jnp.float32
Q_STEPS = (4, 6, 5, 7, 1, 3, 2)
ORDER = (
    ("piece", 3),
    ("halo", 2),
    ("halo", 1),
    ("piece", 1),
    ("piece", 2),
    ("halo", 0),
    ("piece", 0),
)
VMEM_LIMIT = 56 * 2**20


def tables():
    n, m = np.arange(BLOCK), np.arange(BLOCK)
    phase = ((4 * m[:, None] + 1) * n[None, :]) % (4 * BLOCK)
    angle = 2.0 * np.pi * phase / (4 * BLOCK)
    forward = np.concatenate([np.cos(angle), -np.sin(angle)], axis=0)

    def parts(table):
        high = table.astype(ml_dtypes.bfloat16)
        return high, (table - high.astype(np.float64)).astype(ml_dtypes.bfloat16)

    high, low = parts(forward)
    back_high, back_low = parts(forward.T / BLOCK)
    return np.concatenate([high, low], axis=1), np.concatenate([back_high, back_high, back_low], axis=1)


def kernel(
    queries,
    keys,
    values,
    short_filter,
    long_filter,
    skip_gain,
    forward_hbm,
    inverse_hbm,
    q_out,
    r_out,
    key_buf,
    value_buf,
    short_buf,
    filter_buf,
    forward,
    inverse,
    edge_out,
    edge_in,
    edge,
    gated_buf,
    head_buf,
    heads,
    q_raw,
    q_buf,
    signal,
    spectra,
    filter_spectra,
    product,
    result,
    load_sem,
    edge_sem,
    plane_sem,
    gated_send,
    gated_recv,
    head_send,
    head_recv,
    halo_send,
    halo_recv,
    halo_head_send,
    halo_head_recv,
    q_send,
    q_recv,
    q_edge_sem,
    r_send,
    r_recv,
    own_sem,
):
    stretch, grp = lax.axis_index("stretch"), lax.axis_index("grp")
    plane, piece = lax.div(stretch, PIECES), lax.rem(stretch, PIECES)
    half, row = lax.div(grp, 4), lax.rem(grp, 4)
    has_before, has_after = plane > 0, plane < 3
    group_ends = grp == GROUPS - 1
    is_first = jnp.logical_and(stretch == 0, grp == 0)
    is_last = jnp.logical_and(stretch == 15, group_ends)
    next_stretch = lax.rem(stretch + 1, 16)

    def peer(step, sign):
        kp, ky, kx = lax.rem(step, 4), lax.rem(lax.div(step, 4), 4), lax.div(step, 16)
        p = lax.rem(piece + sign * kp + 4, 4)
        y = lax.rem(row + sign * ky + 4, 4)
        h = lax.rem(half + kx, 2)
        return p, h * 4 + y

    def aligned(index, size):
        return pl.ds(pl.multiple_of(index * size, size), size)

    def place(p, g):
        return HALO + 2 * p + lax.div(g, 4), aligned(lax.rem(g, 4), ROWS)

    own_lanes = aligned(piece, LANES)
    loads = [
        pltpu.make_async_copy(keys, key_buf, load_sem.at[0]),
        pltpu.make_async_copy(values, value_buf, load_sem.at[1]),
        pltpu.make_async_copy(short_filter, short_buf, load_sem.at[2]),
        pltpu.make_async_copy(long_filter.at[:, :, own_lanes], filter_buf, load_sem.at[3]),
        pltpu.make_async_copy(forward_hbm, forward, load_sem.at[4]),
        pltpu.make_async_copy(inverse_hbm, inverse, load_sem.at[5]),
    ]
    for load in loads[:5]:
        load.start()

    barrier = pltpu.get_barrier_semaphore()

    def tell(s, g):
        pl.semaphore_signal(barrier, inc=1, device_id=(s, g), device_id_type=MESH)

    for d in range(1, GROUPS):
        tell(stretch, lax.rem(grp + d, GROUPS))
    pieces = [plane * PIECES + lax.rem(piece + d, PIECES) for d in range(1, PIECES)]
    for s in pieces:
        tell(s, grp)

    @pl.when(has_before)
    def _():
        tell(stretch - PIECES, grp)

    @pl.when(jnp.logical_and(has_before, piece == 0))
    def _():
        tell(stretch - 1, grp)

    @pl.when(jnp.logical_and(grp == 0, jnp.logical_not(is_first)))
    def _():
        tell(stretch - 1, GROUPS - 1)

    @pl.when(jnp.logical_not(has_before))
    def _():
        signal[:HALO] = jnp.zeros((HALO, BLOCK, LANES), BF16)

    for load in loads[:3]:
        load.wait()
    fold = 512
    row_at = lax.broadcasted_iota(jnp.int32, (16, fold), 0)
    for n, buf in enumerate((key_buf, value_buf)):
        tail = buf[ROWS - 16 :, :].astype(F32)
        packed = jnp.zeros((16, fold), F32)
        for r in range(2):
            for e in range(8):
                part = tail[14 + r : 15 + r, e * fold : (e + 1) * fold]
                packed = jnp.where(row_at == r * 8 + e, part, packed)
        edge_out[n] = packed.astype(BF16)

    def shorten(now, two, one, position, block):
        at = lax.broadcasted_iota(jnp.int32, now.shape, 0)
        back1 = jnp.where(at == 0, one, pltpu.roll(now, 1, 0))
        back2 = jnp.where(at == 0, two, jnp.where(at == 1, one, pltpu.roll(now, 2, 0)))
        lanes = aligned(block, LANES)
        taps = [short_buf[tap, position : position + 1, lanes] for tap in range(3)]
        return taps[0] * now + taps[1] * back1 + taps[2] * back2

    def block_of(step):
        p, g = peer(step, 1)
        return g * PIECES + p

    def gate_first(step):
        block = block_of(step)
        lanes = aligned(block, LANES)
        factors = [
            shorten(buf[:HEAD, lanes].astype(F32), edge[n, 0:1, lanes], edge[n, 1:2, lanes], n + 1, block)
            for n, buf in enumerate((key_buf, value_buf))
        ]
        head_buf[step] = (factors[0] * factors[1]).astype(BF16)

    def gate_rest(step):
        block = block_of(step)
        lanes = aligned(block, LANES)
        factors = []
        for n, buf in enumerate((key_buf, value_buf)):
            now = buf[:, lanes].astype(F32)
            taps = [short_buf[tap, n + 1 : n + 2, lanes] for tap in range(3)]
            factors.append(taps[0] * now + taps[1] * pltpu.roll(now, 1, 0) + taps[2] * pltpu.roll(now, 2, 0))
        gated_buf[step] = (factors[0] * factors[1])[HEAD:].astype(BF16)

    def gate_ahead(step, carry):
        gate_rest(step)
        return carry

    lax.fori_loop(0, AHEAD, gate_ahead, 0)

    def count(flag):
        return flag.astype(jnp.int32)

    pl.semaphore_wait(
        barrier,
        GROUPS - 1 + PIECES - 1
        + count(has_after)
        + count(jnp.logical_and(has_after, piece == PIECES - 1))
        + count(jnp.logical_and(group_ends, jnp.logical_not(is_last))),
    )
    for s in pieces:
        pl.semaphore_signal(plane_sem, inc=1, device_id=(s, grp), device_id_type=MESH)

    edge_copy = pltpu.make_async_remote_copy(
        edge_out,
        edge_in,
        edge_sem.at[0],
        edge_sem.at[1],
        device_id=(jnp.where(group_ends, next_stretch, stretch), jnp.where(group_ends, 0, grp + 1)),
        device_id_type=MESH,
    )

    @pl.when(jnp.logical_not(is_last))
    def _():
        edge_copy.start()

    def rest_of(p, g):
        block, rows = place(p, g)
        return signal.at[block, pl.ds(pl.multiple_of(rows.start + HEAD, HEAD), ROWS - HEAD)]

    def gated_copy(step):
        p, g = peer(step, 1)
        return pltpu.make_async_remote_copy(
            gated_buf.at[step],
            rest_of(piece, grp),
            gated_send.at[step],
            gated_recv.at[step],
            device_id=(plane * PIECES + p, g),
            device_id_type=MESH,
        )

    def head_copy(step):
        p, g = peer(step, 1)
        return pltpu.make_async_remote_copy(
            head_buf.at[step],
            heads.at[HALO_PIECES + piece, grp],
            head_send.at[step],
            head_recv.at[piece],
            device_id=(plane * PIECES + p, g),
            device_id_type=MESH,
        )

    own_rest = pltpu.make_async_copy(gated_buf.at[0], rest_of(piece, grp), gated_recv.at[0])
    own_rest.start()
    pl.semaphore_wait(plane_sem, PIECES - 1)

    def send_rest(step, carry):
        @pl.when(step >= AHEAD)
        def _():
            gate_rest(step)

        gated_copy(step).start()
        return carry

    lax.fori_loop(1, PEERS, send_rest, 0)

    def q_copy(step):
        other = lax.rem(half + step // 4, 2) * 4 + lax.rem(row + step % 4, 4)
        return pltpu.make_async_remote_copy(
            queries.at[:, aligned(other, 512)],
            q_raw.at[pl.ds(pl.multiple_of(16 + grp * ROWS, 16), ROWS)],
            q_send.at[step],
            q_recv.at[step],
            device_id=(stretch, other),
            device_id_type=MESH,
        )

    own_q = pltpu.make_async_copy(
        queries.at[:, aligned(grp, 512)],
        q_raw.at[pl.ds(pl.multiple_of(16 + grp * ROWS, 16), ROWS)],
        own_sem.at[0],
    )
    own_q.start()

    def transform(source, block, target, rows):
        pair = jnp.concatenate([source[block], source[block + 1]], axis=1)
        bins = jnp.dot(forward[rows, :], jnp.concatenate([pair, pair], axis=0), preferred_element_type=F32)
        target[block, rows] = bins[:, :LANES]
        target[block + 1, rows] = bins[:, LANES:]

    def transform_blocks(source, target, first, pairs):
        def body(unit, carry):
            transform(source, first + 2 * lax.div(unit, 2), target, aligned(lax.rem(unit, 2), BLOCK))
            return carry

        lax.fori_loop(0, 2 * pairs, body, 0)

    @pl.when(is_first)
    def _():
        edge_in[...] = jnp.zeros_like(edge_in)

    @pl.when(jnp.logical_not(is_first))
    def _():
        edge_copy.wait_recv()

    for n in range(2):
        packed = edge_in[n].astype(F32)
        for r in range(2):
            for e in range(8):
                edge[n, r : r + 1, e * fold : (e + 1) * fold] = packed[r * 8 + e : r * 8 + e + 1]

    def send_head(step, carry):
        gate_first(step)
        head_copy(step).start()
        return carry

    lax.fori_loop(1, PEERS, send_head, 0)
    gate_first(0)
    own_head = pltpu.make_async_copy(head_buf.at[0], heads.at[HALO_PIECES + piece, grp], head_recv.at[piece])
    own_head.start()
    loads[5].start()

    def halo_copy(p, g):
        block, rows = place(p, g)
        rest = pl.ds(pl.multiple_of(rows.start + HEAD, HEAD), ROWS - HEAD)
        return pltpu.make_async_remote_copy(
            signal.at[block, rest],
            signal.at[block - OWN, rest],
            halo_send.at[p, g],
            halo_recv.at[p],
            device_id=(lax.rem(stretch + PIECES, 16), grp),
            device_id_type=MESH,
        )

    def halo_head_copy(p):
        return pltpu.make_async_remote_copy(
            heads.at[HALO_PIECES + p],
            heads.at[p - 1],
            halo_head_send.at[p],
            halo_head_recv.at[p],
            device_id=(lax.rem(stretch + PIECES, 16), grp),
            device_id_type=MESH,
        )

    def receive(turn, carry):
        for p in (3, 2, 1, 0):
            step = 4 * turn + lax.rem(piece - p + 4, 4)
            _, g = peer(step, -1)
            rest = rest_of(p, g)
            pltpu.make_async_copy(rest, rest, gated_recv.at[step]).wait()
            if p >= PROMPT:

                @pl.when(has_after)
                def _():
                    halo_copy(p, g).start()

        return carry

    def settle(index, target):
        for c in range(GROUPS):
            signal[target + c // 4, (c % 4) * ROWS : (c % 4) * ROWS + HEAD] = heads[index, c]

    loads[3].wait()
    loads[4].wait()
    transform_blocks(filter_buf, filter_spectra, 0, HALO // 2)

    lax.fori_loop(0, GROUPS, receive, 0)
    for p in (3, 2, 1, 0):
        own_heads = heads.at[HALO_PIECES + p]
        pltpu.make_async_copy(own_heads, own_heads, head_recv.at[p]).wait()
        if p > 0:

            @pl.when(has_after)
            def _(p=p):
                halo_head_copy(p).start()
                if p < PROMPT:
                    for g in range(GROUPS):
                        halo_copy(p, g).start()

    for step in Q_STEPS:
        q_copy(step).start()
    for p in (3, 2, 1, 0):
        settle(HALO_PIECES + p, HALO + 2 * p)
    transform_blocks(signal, spectra, HALO, PIECES)

    gain = skip_gain[own_lanes].reshape(1, LANES)

    def convolve(p):
        def bins(tile, carry):
            real, imag = aligned(tile, 16), pl.ds(pl.multiple_of(BLOCK + tile * 16, 16), 16)
            window = []
            for b in range(HALO + 1):
                here, before = 2 * p + 1 + b, 2 * p + b
                window.append(
                    (
                        spectra[here, real] - spectra[before, imag],
                        spectra[here, imag] + spectra[before, real],
                    )
                )
            sums = [None, None]
            for i in range(HALO):
                fr, fi = filter_spectra[i, real], filter_spectra[i, imag]
                for o in range(2):
                    sr, si = window[HALO - 1 + o - i]
                    re, im = fr * sr - fi * si, fr * si + fi * sr
                    sums[o] = (re, im) if sums[o] is None else (sums[o][0] + re, sums[o][1] + im)
            for n, at_rows in ((0, real), (1, imag)):
                both = jnp.concatenate([sums[0][n], sums[1][n]], axis=1)
                high = both.astype(BF16)
                product[0, at_rows] = high
                product[1, at_rows] = (both - high.astype(F32)).astype(BF16)
            return carry

        lax.fori_loop(0, BLOCK // 16, bins, 0)
        high, low = product[0], product[1]
        back = jnp.dot(inverse[...], jnp.concatenate([high, low, high], axis=0), preferred_element_type=F32)
        for o in range(2):
            direct = gain * signal[HALO + 2 * p + o].astype(F32)
            result[p, pl.ds(o * BLOCK, BLOCK)] = (back[:, o * LANES : (o + 1) * LANES] + direct).astype(BF16)

    def r_copy(p):
        return pltpu.make_async_remote_copy(
            result.at[p],
            r_out.at[:, own_lanes],
            r_send.at[p],
            r_recv.at[piece],
            device_id=(plane * PIECES + p, grp),
            device_id_type=MESH,
        )

    own_r = pltpu.make_async_copy(result.at[piece], r_out.at[:, own_lanes], own_sem.at[1])

    def send_result(p):
        @pl.when(piece != p)
        def _():
            r_copy(p).start()

        @pl.when(piece == p)
        def _():
            own_r.start()

    def halo(p):
        @pl.when(has_before)
        def _():
            rests = signal.at[pl.ds(2 * p, 2), pl.ds(0, 4 * (ROWS - HEAD))]
            pltpu.make_async_copy(rests, rests, halo_recv.at[p + 1]).wait()
            pltpu.make_async_copy(heads.at[p], heads.at[p], halo_head_recv.at[p + 1]).wait()
            settle(p, 2 * p)

        transform_blocks(signal, spectra, 2 * p, 1)

    loads[5].wait()
    for what, p in ORDER:
        if what == "halo":
            halo(p)
        else:
            convolve(p)
            send_result(p)

    own_q.wait()
    for step in range(1, GROUPS):
        q_copy(step).wait_recv()
    q_edge = pltpu.make_async_remote_copy(
        q_raw.at[pl.ds(PIECE, 16)],
        q_raw.at[pl.ds(0, 16)],
        q_edge_sem.at[0],
        q_edge_sem.at[1],
        device_id=(next_stretch, grp),
        device_id_type=MESH,
    )

    @pl.when(stretch < 15)
    def _():
        q_edge.start()

    @pl.when(stretch == 0)
    def _():
        q_raw[:16] = jnp.zeros((16, 512), BF16)

    @pl.when(stretch > 0)
    def _():
        q_edge.wait_recv()

    def shorten_q(unit, carry):
        chunk, part = lax.div(unit, 4), lax.rem(unit, 4)
        lanes = aligned(part, LANES)
        now = q_raw[pl.ds(pl.multiple_of(16 + chunk * ROWS, 16), ROWS), lanes].astype(F32)
        tail = q_raw[aligned(chunk, ROWS), lanes][:16].astype(F32)
        q_buf[aligned(chunk, ROWS), lanes] = shorten(
            now, tail[14:15], tail[15:16], 0, grp * 4 + part
        ).astype(BF16)
        return carry

    lax.fori_loop(0, 32, shorten_q, 0)
    q_copy_out = pltpu.make_async_copy(q_buf, q_out, own_sem.at[0])
    q_copy_out.start()

    q_copy_out.wait()
    own_r.wait()
    for p in range(PIECES):

        @pl.when(piece != p)
        def _(p=p):
            r_copy(p).wait_send()
            lanes = pl.ds(p * LANES, LANES)
            pltpu.make_async_copy(r_out.at[:, lanes], r_out.at[:, lanes], r_recv.at[p]).wait()

    for step in range(1, GROUPS):
        q_copy(step).wait_send()

    @pl.when(stretch < 15)
    def _():
        q_edge.wait_send()

    @pl.when(jnp.logical_not(is_last))
    def _():
        edge_copy.wait_send()

    def sent(step, carry):
        gated_copy(step).wait_send()
        head_copy(step).wait_send()
        return carry

    lax.fori_loop(1, PEERS, sent, 0)

    @pl.when(has_after)
    def _():
        for p in range(1, PIECES):
            halo_head_copy(p).wait_send()

            def halo_sent(g, carry, p=p):
                halo_copy(p, g).wait_send()
                return carry

            lax.fori_loop(0, GROUPS, halo_sent, 0)


def local(queries, keys, values, short_filter, long_filter, skip_gain):
    width = queries.shape[1]
    slice_width = width // GROUPS
    forward, inverse = tables()
    hbm, vmem = pl.BlockSpec(memory_space=pltpu.HBM), pl.BlockSpec(memory_space=pltpu.VMEM)
    anywhere = pl.BlockSpec(memory_space=pl.ANY)
    dma = pltpu.SemaphoreType.DMA
    q_slices, convolved = pl.pallas_call(
        kernel,
        out_shape=[jax.ShapeDtypeStruct((PIECE, slice_width), BF16)] * 2,
        in_specs=[hbm, hbm, hbm, hbm, hbm, vmem, hbm, hbm],
        out_specs=[anywhere, anywhere],
        scratch_shapes=[
            pltpu.VMEM((ROWS, width), BF16),
            pltpu.VMEM((ROWS, width), BF16),
            pltpu.VMEM((3, 3, width), F32),
            pltpu.VMEM((HALO, BLOCK, LANES), BF16),
            pltpu.VMEM(forward.shape, BF16),
            pltpu.VMEM(inverse.shape, BF16),
            pltpu.VMEM((2, 16, 512), BF16),
            pltpu.VMEM((2, 16, 512), BF16),
            pltpu.VMEM((2, 8, width), F32),
            pltpu.VMEM((PEERS, ROWS - HEAD, LANES), BF16),
            pltpu.VMEM((PEERS, HEAD, LANES), BF16),
            pltpu.VMEM((HALO_PIECES + PIECES, GROUPS, HEAD, LANES), BF16),
            pltpu.VMEM((16 + PIECE, slice_width), BF16),
            pltpu.VMEM((PIECE, slice_width), BF16),
            pltpu.VMEM((HALO + OWN, BLOCK, LANES), BF16),
            pltpu.VMEM((HALO + OWN, 2 * BLOCK, LANES), F32),
            pltpu.VMEM((HALO, 2 * BLOCK, LANES), F32),
            pltpu.VMEM((2, 2 * BLOCK, 2 * LANES), BF16),
            pltpu.VMEM((PIECES, PIECE, LANES), BF16),
            dma((6,)),
            dma((2,)),
            pltpu.SemaphoreType.REGULAR,
            dma((PEERS,)),
            dma((PEERS,)),
            dma((PEERS,)),
            dma((PIECES,)),
            dma((PIECES, GROUPS)),
            dma((PIECES,)),
            dma((PIECES,)),
            dma((PIECES,)),
            dma((GROUPS,)),
            dma((GROUPS,)),
            dma((2,)),
            dma((PIECES,)),
            dma((PIECES,)),
            dma((2,)),
        ],
        compiler_params=pltpu.CompilerParams(
            collective_id=0, has_side_effects=True, vmem_limit_bytes=VMEM_LIMIT
        ),
        cost_estimate=pl.CostEstimate(flops=9 * 10**9, bytes_accessed=16 * 2**20, transcendentals=0),
    )(
        queries,
        keys,
        values,
        short_filter,
        long_filter.reshape(HALO, BLOCK, slice_width),
        skip_gain,
        jnp.asarray(forward),
        jnp.asarray(inverse),
    )
    return (q_slices.astype(F32) * convolved.astype(F32)).astype(BF16)


def solution(mesh):
    return jax.shard_map(
        local,
        mesh=mesh,
        in_specs=(
            P(("stretch", "grp"), None),
            P(("stretch", "grp"), None),
            P(("stretch", "grp"), None),
            P(),
            P(None, "grp"),
            P("grp"),
        ),
        out_specs=P("stretch", "grp"),
        check_vma=False,
    )
```

```python
import jax
import jax.numpy as jnp
import ml_dtypes
import numpy as np
from jax import lax
from jax.experimental import pallas as pl
from jax.experimental.pallas import tpu as pltpu
from jax.sharding import PartitionSpec as P

MESH = pl.DeviceIdType.MESH
BLOCK = 512
LANES = 128
ROWS = 128
HEAD = 16
PIECES = 4
GROUPS = 8
PEERS = PIECES * GROUPS
PIECE = ROWS * GROUPS
TAPS = 3072
HALO = TAPS // BLOCK
OWN = PIECES * PIECE // BLOCK
HALO_PIECES = TAPS // PIECE
AHEAD = 16
PROMPT = 2
BF16, F32 = jnp.bfloat16, jnp.float32
FAR = ((), (0, 2, 1, 3), (), (), (), (), (), ())
NEAR = ((), (1, 3, 2), (), (), (), (), (), ())
ORDER = (
    ("piece", 3),
    ("halo", 2),
    ("halo", 1),
    ("piece", 1),
    ("piece", 2),
    ("halo", 0),
    ("piece", 0),
)
VMEM_LIMIT = 56 * 2**20


def tables():
    n, m = np.arange(BLOCK), np.arange(BLOCK)
    phase = ((4 * m[:, None] + 1) * n[None, :]) % (4 * BLOCK)
    angle = 2.0 * np.pi * phase / (4 * BLOCK)
    forward = np.concatenate([np.cos(angle), -np.sin(angle)], axis=0)

    def parts(table):
        high = table.astype(ml_dtypes.bfloat16)
        return high, (table - high.astype(np.float64)).astype(ml_dtypes.bfloat16)

    high, low = parts(forward)
    back_high, back_low = parts(forward.T / BLOCK)
    return np.concatenate([high, low], axis=1), np.concatenate([back_high, back_high, back_low], axis=1)


def kernel(
    queries,
    keys,
    values,
    short_filter,
    long_filter,
    skip_gain,
    forward_hbm,
    inverse_hbm,
    q_out,
    r_out,
    key_buf,
    value_buf,
    query_buf,
    short_buf,
    filter_buf,
    forward,
    inverse,
    edge_out,
    edge_in,
    edge,
    gated_buf,
    head_buf,
    heads,
    q_buf,
    q_mid,
    ones,
    signal,
    spectra,
    filter_spectra,
    product,
    result,
    load_sem,
    edge_sem,
    plane_sem,
    gated_send,
    gated_recv,
    head_send,
    head_recv,
    halo_send,
    halo_recv,
    halo_head_send,
    halo_head_recv,
    q_send,
    q_recv,
    q_mid_send,
    q_mid_recv,
    r_send,
    r_recv,
    own_sem,
):
    stretch, grp = lax.axis_index("stretch"), lax.axis_index("grp")
    plane, piece = lax.div(stretch, PIECES), lax.rem(stretch, PIECES)
    half, row = lax.div(grp, 4), lax.rem(grp, 4)
    side, core = lax.div(piece, 2), lax.rem(piece, 2)
    has_before, has_after = plane > 0, plane < 3
    group_ends = grp == GROUPS - 1
    is_first = jnp.logical_and(stretch == 0, grp == 0)
    is_last = jnp.logical_and(stretch == 15, group_ends)

    def peer(step, sign):
        kp, ky, kx = lax.rem(step, 4), lax.div(step, 8), lax.rem(lax.div(step, 4), 2)
        p = lax.rem(piece + sign * kp + 4, 4)
        sender = core if sign > 0 else lax.rem(p, 2)
        y = lax.rem(row + sign * ky * (1 - 2 * sender) + 4, 4)
        h = lax.rem(half + kx, 2)
        return p, h * 4 + y

    def aligned(index, size):
        return pl.ds(pl.multiple_of(index * size, size), size)

    def place(p, g):
        return HALO + 2 * p + lax.div(g, 4), aligned(lax.rem(g, 4), ROWS)

    own_lanes = aligned(piece, LANES)
    loads = [
        pltpu.make_async_copy(keys, key_buf, load_sem.at[0]),
        pltpu.make_async_copy(values, value_buf, load_sem.at[1]),
        pltpu.make_async_copy(short_filter, short_buf, load_sem.at[2]),
        pltpu.make_async_copy(long_filter.at[:, :, own_lanes], filter_buf, load_sem.at[3]),
        pltpu.make_async_copy(forward_hbm, forward, load_sem.at[4]),
        pltpu.make_async_copy(inverse_hbm, inverse, load_sem.at[5]),
        pltpu.make_async_copy(queries, query_buf, load_sem.at[6]),
    ]
    for load in loads[:3] + loads[6:] + loads[3:5]:
        load.start()

    barrier = pltpu.get_barrier_semaphore()

    def tell(s, g):
        pl.semaphore_signal(barrier, inc=1, device_id=(s, g), device_id_type=MESH)

    for d in range(1, GROUPS):
        tell(stretch, lax.rem(grp + d, GROUPS))
    pieces = [plane * PIECES + lax.rem(piece + d, PIECES) for d in range(1, PIECES)]
    for s in pieces:
        tell(s, grp)

    @pl.when(has_before)
    def _():
        tell(stretch - PIECES, grp)

    @pl.when(jnp.logical_and(grp == 0, jnp.logical_not(is_first)))
    def _():
        tell(stretch - 1, GROUPS - 1)

    @pl.when(jnp.logical_not(has_before))
    def _():
        signal[:HALO] = jnp.zeros((HALO, BLOCK, LANES), BF16)

    for load in loads[:3]:
        load.wait()
    loads[6].wait()
    fold = 512
    row_at = lax.broadcasted_iota(jnp.int32, (16, fold), 0)
    for n, buf in enumerate((key_buf, value_buf, query_buf)):
        tail = buf[ROWS - 16 :, :].astype(F32)
        packed = jnp.zeros((16, fold), F32)
        for r in range(2):
            for e in range(8):
                part = tail[14 + r : 15 + r, e * fold : (e + 1) * fold]
                packed = jnp.where(row_at == r * 8 + e, part, packed)
        edge_out[n] = packed.astype(BF16)

    def shorten(now, two, one, position, block):
        at = lax.broadcasted_iota(jnp.int32, now.shape, 0)
        back1 = jnp.where(at == 0, one, pltpu.roll(now, 1, 0))
        back2 = jnp.where(at == 0, two, jnp.where(at == 1, one, pltpu.roll(now, 2, 0)))
        lanes = aligned(block, LANES)
        taps = [short_buf[tap, position : position + 1, lanes] for tap in range(3)]
        return taps[0] * now + taps[1] * back1 + taps[2] * back2

    def block_of(step):
        p, g = peer(step, 1)
        return g * PIECES + p

    def gate_first(step):
        block = block_of(step)
        lanes = aligned(block, LANES)
        factors = [
            shorten(buf[:HEAD, lanes].astype(F32), edge[n, 0:1, lanes], edge[n, 1:2, lanes], n + 1, block)
            for n, buf in enumerate((key_buf, value_buf))
        ]
        head_buf[step] = (factors[0] * factors[1]).astype(BF16)

    def gate_rest(step):
        block = block_of(step)
        lanes = aligned(block, LANES)
        factors = []
        for n, buf in enumerate((key_buf, value_buf)):
            now = buf[:, lanes].astype(F32)
            taps = [short_buf[tap, n + 1 : n + 2, lanes] for tap in range(3)]
            factors.append(taps[0] * now + taps[1] * pltpu.roll(now, 1, 0) + taps[2] * pltpu.roll(now, 2, 0))
        gated_buf[step] = (factors[0] * factors[1])[HEAD:].astype(BF16)

    def gate_ahead(step, carry):
        gate_rest(step)
        return carry

    lax.fori_loop(0, AHEAD, gate_ahead, 0)

    def count(flag):
        return flag.astype(jnp.int32)

    pl.semaphore_wait(
        barrier,
        GROUPS - 1 + PIECES - 1
        + count(has_after)
        + count(jnp.logical_and(group_ends, jnp.logical_not(is_last))),
    )
    for s in pieces:
        pl.semaphore_signal(plane_sem, inc=1, device_id=(s, grp), device_id_type=MESH)

    edge_copy = pltpu.make_async_remote_copy(
        edge_out,
        edge_in,
        edge_sem.at[0],
        edge_sem.at[1],
        device_id=(jnp.where(group_ends, lax.rem(stretch + 1, 16), stretch), jnp.where(group_ends, 0, grp + 1)),
        device_id_type=MESH,
    )

    @pl.when(jnp.logical_not(is_last))
    def _():
        edge_copy.start()

    def rest_of(p, g):
        block, rows = place(p, g)
        return signal.at[block, pl.ds(pl.multiple_of(rows.start + HEAD, HEAD), ROWS - HEAD)]

    def gated_copy(step):
        p, g = peer(step, 1)
        return pltpu.make_async_remote_copy(
            gated_buf.at[step],
            rest_of(piece, grp),
            gated_send.at[step],
            gated_recv.at[step],
            device_id=(plane * PIECES + p, g),
            device_id_type=MESH,
        )

    def head_copy(step):
        p, g = peer(step, 1)
        return pltpu.make_async_remote_copy(
            head_buf.at[step],
            heads.at[HALO_PIECES + piece, grp],
            head_send.at[step],
            head_recv.at[piece],
            device_id=(plane * PIECES + p, g),
            device_id_type=MESH,
        )

    own_rest = pltpu.make_async_copy(gated_buf.at[0], rest_of(piece, grp), gated_recv.at[0])
    own_rest.start()
    pl.semaphore_wait(plane_sem, PIECES - 1)

    def send_rest(step, carry):
        @pl.when(step >= AHEAD)
        def _():
            gate_rest(step)

        gated_copy(step).start()
        return carry

    lax.fori_loop(1, PEERS, send_rest, 0)

    def transform(source, block, target, rows):
        pair = jnp.concatenate([source[block], source[block + 1]], axis=1)
        bins = jnp.dot(forward[rows, :], jnp.concatenate([pair, pair], axis=0), preferred_element_type=F32)
        target[block, rows] = bins[:, :LANES]
        target[block + 1, rows] = bins[:, LANES:]

    def transform_blocks(source, target, first, pairs):
        def body(unit, carry):
            transform(source, first + 2 * lax.div(unit, 2), target, aligned(lax.rem(unit, 2), BLOCK))
            return carry

        lax.fori_loop(0, 2 * pairs, body, 0)

    @pl.when(is_first)
    def _():
        edge_in[...] = jnp.zeros_like(edge_in)

    @pl.when(jnp.logical_not(is_first))
    def _():
        edge_copy.wait_recv()

    for n in range(3):
        packed = edge_in[n].astype(F32)
        for r in range(2):
            for e in range(8):
                edge[n, r : r + 1, e * fold : (e + 1) * fold] = packed[r * 8 + e : r * 8 + e + 1]

    def send_head(step, carry):
        gate_first(step)
        head_copy(step).start()
        return carry

    lax.fori_loop(1, PEERS, send_head, 0)
    gate_first(0)
    own_head = pltpu.make_async_copy(head_buf.at[0], heads.at[HALO_PIECES + piece, grp], head_recv.at[piece])
    own_head.start()

    def shorten_q(block, carry):
        lanes = aligned(block, LANES)
        now = query_buf[:, lanes].astype(F32)
        q_buf[:, lanes] = shorten(now, edge[2, 0:1, lanes], edge[2, 1:2, lanes], 0, block).astype(BF16)
        return carry

    lax.fori_loop(0, PEERS, shorten_q, 0)
    ones[...] = jnp.ones_like(ones)
    q_rows = aligned(grp, ROWS)
    side_lanes = aligned(side, 2 * LANES)
    own_q = pltpu.make_async_copy(q_buf.at[:, aligned(grp, 512)], q_out.at[q_rows], own_sem.at[0])
    ones_copy = pltpu.make_async_copy(
        ones, q_out.at[aligned(1 - half, BLOCK), aligned(1 - side, 2 * LANES)], own_sem.at[2]
    )

    def q_near(step):
        other = half * 4 + lax.rem(row + step, 4)
        return pltpu.make_async_remote_copy(
            q_buf.at[:, aligned(other, 512)],
            q_out.at[q_rows],
            q_send.at[step],
            q_recv.at[step],
            device_id=(stretch, other),
            device_id_type=MESH,
        )

    def q_far(step):
        other = (1 - half) * 4 + lax.rem(row + step, 4)
        return pltpu.make_async_remote_copy(
            q_buf.at[:, aligned(other * 2 + side, 2 * LANES)],
            q_out.at[q_rows, side_lanes],
            q_send.at[4 + step],
            q_recv.at[4 + step],
            device_id=(stretch, other),
            device_id_type=MESH,
        )

    def q_aside(step):
        k = step % 2
        other, p = (1 - half) * 4 + lax.rem(row + step // 2, 4), 2 * (1 - side) + k
        return pltpu.make_async_remote_copy(
            q_buf.at[:, aligned(other * PIECES + p, LANES)],
            q_mid.at[core, aligned(row, ROWS)],
            q_mid_send.at[step],
            q_mid_recv.at[core],
            device_id=(plane * PIECES + p, other),
            device_id_type=MESH,
        )

    for step in range(8):
        q_aside(step).start()

    def send_q(turn):
        for step in FAR[turn]:
            q_far(step).start()
        for step in NEAR[turn]:
            q_near(step).start()

    own_q.start()
    ones_copy.start()

    loads[5].start()

    def halo_copy(p, g):
        block, rows = place(p, g)
        rest = pl.ds(pl.multiple_of(rows.start + HEAD, HEAD), ROWS - HEAD)
        return pltpu.make_async_remote_copy(
            signal.at[block, rest],
            signal.at[block - OWN, rest],
            halo_send.at[p, g],
            halo_recv.at[p],
            device_id=(lax.rem(stretch + PIECES, 16), grp),
            device_id_type=MESH,
        )

    def halo_head_copy(p):
        return pltpu.make_async_remote_copy(
            heads.at[HALO_PIECES + p],
            heads.at[p - 1],
            halo_head_send.at[p],
            halo_head_recv.at[p],
            device_id=(lax.rem(stretch + PIECES, 16), grp),
            device_id_type=MESH,
        )

    def receive(turn, carry):
        for p in (3, 2, 1, 0):
            step = 4 * turn + lax.rem(piece - p + 4, 4)
            _, g = peer(step, -1)
            rest = rest_of(p, g)
            pltpu.make_async_copy(rest, rest, gated_recv.at[step]).wait()
            if p >= PROMPT:

                @pl.when(has_after)
                def _():
                    halo_copy(p, g).start()

        return carry

    def settle(index, target):
        for c in range(GROUPS):
            signal[target + c // 4, (c % 4) * ROWS : (c % 4) * ROWS + HEAD] = heads[index, c]

    loads[3].wait()
    loads[4].wait()
    transform_blocks(filter_buf, filter_spectra, 0, HALO // 2)

    lax.fori_loop(0, GROUPS, receive, 0)
    for p in (3, 2, 1, 0):
        own_heads = heads.at[HALO_PIECES + p]
        pltpu.make_async_copy(own_heads, own_heads, head_recv.at[p]).wait()
        if p > 0:

            @pl.when(has_after)
            def _(p=p):
                halo_head_copy(p).start()
                if p < PROMPT:
                    for g in range(GROUPS):
                        halo_copy(p, g).start()

    send_q(0)
    for p in (3, 2, 1, 0):
        settle(HALO_PIECES + p, HALO + 2 * p)
    transform_blocks(signal, spectra, HALO, PIECES)

    gain = skip_gain[own_lanes].reshape(1, LANES)

    def wait_q_mid():
        for c in range(2):
            pltpu.make_async_copy(q_mid.at[c], q_mid.at[c], q_mid_recv.at[c]).wait()

    def convolve(p, first):
        def bins(tile, carry):
            real, imag = aligned(tile, 16), pl.ds(pl.multiple_of(BLOCK + tile * 16, 16), 16)
            window = []
            for b in range(HALO + 1):
                here, before = 2 * p + 1 + b, 2 * p + b
                window.append(
                    (
                        spectra[here, real] - spectra[before, imag],
                        spectra[here, imag] + spectra[before, real],
                    )
                )
            sums = [None, None]
            for i in range(HALO):
                fr, fi = filter_spectra[i, real], filter_spectra[i, imag]
                for o in range(2):
                    sr, si = window[HALO - 1 + o - i]
                    re, im = fr * sr - fi * si, fr * si + fi * sr
                    sums[o] = (re, im) if sums[o] is None else (sums[o][0] + re, sums[o][1] + im)
            for n, at_rows in ((0, real), (1, imag)):
                both = jnp.concatenate([sums[0][n], sums[1][n]], axis=1)
                high = both.astype(BF16)
                product[0, at_rows] = high
                product[1, at_rows] = (both - high.astype(F32)).astype(BF16)
            return carry

        lax.fori_loop(0, BLOCK // 16, bins, 0)
        high, low = product[0], product[1]
        back = jnp.dot(inverse[...], jnp.concatenate([high, low, high], axis=0), preferred_element_type=F32)
        for o in range(2):
            direct = gain * signal[HALO + 2 * p + o].astype(F32)
            total = back[:, o * LANES : (o + 1) * LANES] + direct
            here = jnp.logical_and(side != p // 2, half != o)

            @pl.when(here)
            def _():
                if first:
                    wait_q_mid()
                result[p, pl.ds(o * BLOCK, BLOCK)] = (total * q_mid[p % 2].astype(F32)).astype(BF16)

            @pl.when(jnp.logical_not(here))
            def _():
                result[p, pl.ds(o * BLOCK, BLOCK)] = total.astype(BF16)


    def r_copy(p):
        return pltpu.make_async_remote_copy(
            result.at[p],
            r_out.at[:, own_lanes],
            r_send.at[p],
            r_recv.at[piece],
            device_id=(plane * PIECES + p, grp),
            device_id_type=MESH,
        )

    own_r = pltpu.make_async_copy(result.at[piece], r_out.at[:, own_lanes], own_sem.at[1])

    def send_result(p):
        @pl.when(piece != p)
        def _():
            r_copy(p).start()

        @pl.when(piece == p)
        def _():
            own_r.start()

    def halo(p):
        @pl.when(has_before)
        def _():
            rests = signal.at[pl.ds(2 * p, 2), pl.ds(0, 4 * (ROWS - HEAD))]
            pltpu.make_async_copy(rests, rests, halo_recv.at[p + 1]).wait()
            pltpu.make_async_copy(heads.at[p], heads.at[p], halo_head_recv.at[p + 1]).wait()
            settle(p, 2 * p)

        transform_blocks(signal, spectra, 2 * p, 1)

    loads[5].wait()
    sides = set()
    for turn, (what, p) in enumerate(ORDER):
        if what == "halo":
            halo(p)
        else:
            convolve(p, p // 2 not in sides)
            sides.add(p // 2)
            send_result(p)
        send_q(1 + turn)

    own_q.wait()
    ones_copy.wait()
    own_r.wait()
    for p in range(PIECES):

        @pl.when(piece != p)
        def _(p=p):
            r_copy(p).wait_send()
            lanes = pl.ds(p * LANES, LANES)
            pltpu.make_async_copy(r_out.at[:, lanes], r_out.at[:, lanes], r_recv.at[p]).wait()

    for step in range(1, 4):
        q_near(step).wait()
    for step in range(4):
        q_far(step).wait()
    for step in range(8):
        q_aside(step).wait_send()

    @pl.when(jnp.logical_not(is_last))
    def _():
        edge_copy.wait_send()

    def sent(step, carry):
        gated_copy(step).wait_send()
        head_copy(step).wait_send()
        return carry

    lax.fori_loop(1, PEERS, sent, 0)

    @pl.when(has_after)
    def _():
        for p in range(1, PIECES):
            halo_head_copy(p).wait_send()

            def halo_sent(g, carry, p=p):
                halo_copy(p, g).wait_send()
                return carry

            lax.fori_loop(0, GROUPS, halo_sent, 0)


def multiply(q_ref, r_ref, out_ref):
    out_ref[...] = (q_ref[...].astype(F32) * r_ref[...].astype(F32)).astype(BF16)


def local(queries, keys, values, short_filter, long_filter, skip_gain):
    width = queries.shape[1]
    slice_width = width // GROUPS
    forward, inverse = tables()
    hbm, vmem = pl.BlockSpec(memory_space=pltpu.HBM), pl.BlockSpec(memory_space=pltpu.VMEM)
    anywhere = pl.BlockSpec(memory_space=pl.ANY)
    dma = pltpu.SemaphoreType.DMA
    q_slices, convolved = pl.pallas_call(
        kernel,
        out_shape=[jax.ShapeDtypeStruct((PIECE, slice_width), BF16)] * 2,
        in_specs=[hbm, hbm, hbm, hbm, hbm, vmem, hbm, hbm],
        out_specs=[anywhere, anywhere],
        scratch_shapes=[
            pltpu.VMEM((ROWS, width), BF16),
            pltpu.VMEM((ROWS, width), BF16),
            pltpu.VMEM((ROWS, width), BF16),
            pltpu.VMEM((3, 3, width), F32),
            pltpu.VMEM((HALO, BLOCK, LANES), BF16),
            pltpu.VMEM(forward.shape, BF16),
            pltpu.VMEM(inverse.shape, BF16),
            pltpu.VMEM((3, 16, 512), BF16),
            pltpu.VMEM((3, 16, 512), BF16),
            pltpu.VMEM((3, 8, width), F32),
            pltpu.VMEM((PEERS, ROWS - HEAD, LANES), BF16),
            pltpu.VMEM((PEERS, HEAD, LANES), BF16),
            pltpu.VMEM((HALO_PIECES + PIECES, GROUPS, HEAD, LANES), BF16),
            pltpu.VMEM((ROWS, width), BF16),
            pltpu.VMEM((2, BLOCK, LANES), BF16),
            pltpu.VMEM((BLOCK, 2 * LANES), BF16),
            pltpu.VMEM((HALO + OWN, BLOCK, LANES), BF16),
            pltpu.VMEM((HALO + OWN, 2 * BLOCK, LANES), F32),
            pltpu.VMEM((HALO, 2 * BLOCK, LANES), F32),
            pltpu.VMEM((2, 2 * BLOCK, 2 * LANES), BF16),
            pltpu.VMEM((PIECES, PIECE, LANES), BF16),
            dma((7,)),
            dma((2,)),
            pltpu.SemaphoreType.REGULAR,
            dma((PEERS,)),
            dma((PEERS,)),
            dma((PEERS,)),
            dma((PIECES,)),
            dma((PIECES, GROUPS)),
            dma((PIECES,)),
            dma((PIECES,)),
            dma((PIECES,)),
            dma((GROUPS,)),
            dma((GROUPS,)),
            dma((8,)),
            dma((2,)),
            dma((PIECES,)),
            dma((PIECES,)),
            dma((3,)),
        ],
        compiler_params=pltpu.CompilerParams(
            collective_id=0, has_side_effects=True, vmem_limit_bytes=VMEM_LIMIT
        ),
        cost_estimate=pl.CostEstimate(flops=9 * 10**9, bytes_accessed=16 * 2**20, transcendentals=0),
    )(
        queries,
        keys,
        values,
        short_filter,
        long_filter.reshape(HALO, BLOCK, slice_width),
        skip_gain,
        jnp.asarray(forward),
        jnp.asarray(inverse),
    )
    rows = PIECE // 2
    part = pl.BlockSpec((rows, slice_width), lambda i: (i, 0))
    return pl.pallas_call(
        multiply,
        out_shape=jax.ShapeDtypeStruct((PIECE, slice_width), BF16),
        grid=(2,),
        in_specs=[part, part],
        out_specs=part,
    )(q_slices, convolved)


def solution(mesh):
    return jax.shard_map(
        local,
        mesh=mesh,
        in_specs=(
            P(("stretch", "grp"), None),
            P(("stretch", "grp"), None),
            P(("stretch", "grp"), None),
            P(),
            P(None, "grp"),
            P("grp"),
        ),
        out_specs=P("stretch", "grp"),
        check_vma=False,
    )
```

```python
import jax
import jax.numpy as jnp
import ml_dtypes
import numpy as np
from jax import lax
from jax.experimental import pallas as pl
from jax.experimental.pallas import tpu as pltpu
from jax.sharding import PartitionSpec as P

MESH = pl.DeviceIdType.MESH
BLOCK = 512
LANES = 128
ROWS = 128
HEAD = 16
PIECES = 4
GROUPS = 8
PEERS = PIECES * GROUPS
PIECE = ROWS * GROUPS
TAPS = 3072
HALO = TAPS // BLOCK
OWN = PIECES * PIECE // BLOCK
HALO_PIECES = TAPS // PIECE
AHEAD = 8
PROMPT = 2
BF16, F32 = jnp.bfloat16, jnp.float32
FAR = ((0, 2), (1, 3), (), (), (), (), (), ())
NEAR = ((1, 3, 2), (), (), (), (), (), (), ())
ORDER = (
    ("piece", 3),
    ("halo", 2),
    ("halo", 1),
    ("piece", 1),
    ("piece", 2),
    ("halo", 0),
    ("piece", 0),
)
VMEM_LIMIT = 56 * 2**20


def tables():
    n, m = np.arange(BLOCK), np.arange(BLOCK)
    phase = ((4 * m[:, None] + 1) * n[None, :]) % (4 * BLOCK)
    angle = 2.0 * np.pi * phase / (4 * BLOCK)
    forward = np.concatenate([np.cos(angle), -np.sin(angle)], axis=0)

    def parts(table):
        high = table.astype(ml_dtypes.bfloat16)
        return high, (table - high.astype(np.float64)).astype(ml_dtypes.bfloat16)

    high, low = parts(forward)
    back_high, back_low = parts(forward.T / BLOCK)
    return np.concatenate([high, low], axis=1), np.concatenate([back_high, back_high, back_low], axis=1)


def kernel(
    queries,
    keys,
    values,
    short_filter,
    long_filter,
    skip_gain,
    forward_hbm,
    inverse_hbm,
    q_out,
    r_out,
    key_buf,
    value_buf,
    query_buf,
    short_buf,
    filter_buf,
    forward,
    inverse,
    edge_out,
    edge_in,
    edge,
    gated_buf,
    head_buf,
    heads,
    q_buf,
    q_mid,
    ones,
    signal,
    spectra,
    filter_spectra,
    product,
    result,
    load_sem,
    edge_sem,
    plane_sem,
    gated_send,
    gated_recv,
    head_send,
    head_recv,
    halo_send,
    halo_recv,
    halo_head_send,
    halo_head_recv,
    q_send,
    q_recv,
    q_mid_send,
    q_mid_recv,
    r_send,
    r_recv,
    own_sem,
):
    stretch, grp = lax.axis_index("stretch"), lax.axis_index("grp")
    plane, piece = lax.div(stretch, PIECES), lax.rem(stretch, PIECES)
    half, row = lax.div(grp, 4), lax.rem(grp, 4)
    side, core = lax.div(piece, 2), lax.rem(piece, 2)
    around = 1 - 2 * core
    has_before, has_after = plane > 0, plane < 3
    group_ends = grp == GROUPS - 1
    is_first = jnp.logical_and(stretch == 0, grp == 0)
    is_last = jnp.logical_and(stretch == 15, group_ends)

    def peer(step, sign):
        kp, ky, kx = lax.rem(step, 4), lax.div(step, 8), lax.rem(lax.div(step, 4), 2)
        p = lax.rem(piece + sign * kp + 4, 4)
        sender = core if sign > 0 else lax.rem(p, 2)
        y = lax.rem(row + sign * ky * (1 - 2 * sender) + 4, 4)
        h = lax.rem(half + kx, 2)
        return p, h * 4 + y

    def aligned(index, size):
        return pl.ds(pl.multiple_of(index * size, size), size)

    def place(p, g):
        return HALO + 2 * p + lax.div(g, 4), aligned(lax.rem(g, 4), ROWS)

    own_lanes = aligned(piece, LANES)
    loads = [
        pltpu.make_async_copy(keys, key_buf, load_sem.at[0]),
        pltpu.make_async_copy(values, value_buf, load_sem.at[1]),
        pltpu.make_async_copy(short_filter, short_buf, load_sem.at[2]),
        pltpu.make_async_copy(long_filter.at[:, :, own_lanes], filter_buf, load_sem.at[3]),
        pltpu.make_async_copy(forward_hbm, forward, load_sem.at[4]),
        pltpu.make_async_copy(inverse_hbm, inverse, load_sem.at[5]),
        pltpu.make_async_copy(queries, query_buf, load_sem.at[6]),
    ]
    for load in loads[:3] + loads[6:] + loads[3:5]:
        load.start()

    barrier = pltpu.get_barrier_semaphore()

    def tell(s, g):
        pl.semaphore_signal(barrier, inc=1, device_id=(s, g), device_id_type=MESH)

    for d in range(1, GROUPS):
        tell(stretch, lax.rem(grp + d, GROUPS))
    pieces = [plane * PIECES + lax.rem(piece + d, PIECES) for d in range(1, PIECES)]
    for s in pieces:
        tell(s, grp)

    @pl.when(has_before)
    def _():
        tell(stretch - PIECES, grp)

    @pl.when(jnp.logical_and(grp == 0, jnp.logical_not(is_first)))
    def _():
        tell(stretch - 1, GROUPS - 1)

    @pl.when(jnp.logical_not(has_before))
    def _():
        signal[:HALO] = jnp.zeros((HALO, BLOCK, LANES), BF16)

    for load in loads[:3]:
        load.wait()
    loads[6].wait()
    fold = 512
    row_at = lax.broadcasted_iota(jnp.int32, (16, fold), 0)
    for n, buf in enumerate((key_buf, value_buf, query_buf)):
        tail = buf[ROWS - 16 :, :].astype(F32)
        packed = jnp.zeros((16, fold), F32)
        for r in range(2):
            for e in range(8):
                part = tail[14 + r : 15 + r, e * fold : (e + 1) * fold]
                packed = jnp.where(row_at == r * 8 + e, part, packed)
        edge_out[n] = packed.astype(BF16)

    def shorten(now, two, one, position, block):
        at = lax.broadcasted_iota(jnp.int32, now.shape, 0)
        back1 = jnp.where(at == 0, one, pltpu.roll(now, 1, 0))
        back2 = jnp.where(at == 0, two, jnp.where(at == 1, one, pltpu.roll(now, 2, 0)))
        lanes = aligned(block, LANES)
        taps = [short_buf[tap, position : position + 1, lanes] for tap in range(3)]
        return taps[0] * now + taps[1] * back1 + taps[2] * back2

    def block_of(step):
        p, g = peer(step, 1)
        return g * PIECES + p

    def gate_first(step):
        block = block_of(step)
        lanes = aligned(block, LANES)
        factors = [
            shorten(buf[:HEAD, lanes].astype(F32), edge[n, 0:1, lanes], edge[n, 1:2, lanes], n + 1, block)
            for n, buf in enumerate((key_buf, value_buf))
        ]
        head_buf[step] = (factors[0] * factors[1]).astype(BF16)

    def gate_rest(step):
        block = block_of(step)
        lanes = aligned(block, LANES)
        factors = []
        for n, buf in enumerate((key_buf, value_buf)):
            now = buf[:, lanes].astype(F32)
            taps = [short_buf[tap, n + 1 : n + 2, lanes] for tap in range(3)]
            factors.append(taps[0] * now + taps[1] * pltpu.roll(now, 1, 0) + taps[2] * pltpu.roll(now, 2, 0))
        gated_buf[step] = (factors[0] * factors[1])[HEAD:].astype(BF16)

    def gate_ahead(step, carry):
        gate_rest(step)
        return carry

    lax.fori_loop(0, AHEAD, gate_ahead, 0)

    def count(flag):
        return flag.astype(jnp.int32)

    pl.semaphore_wait(
        barrier,
        GROUPS - 1 + PIECES - 1
        + count(has_after)
        + count(jnp.logical_and(group_ends, jnp.logical_not(is_last))),
    )
    for s in pieces:
        pl.semaphore_signal(plane_sem, inc=1, device_id=(s, grp), device_id_type=MESH)

    edge_copy = pltpu.make_async_remote_copy(
        edge_out,
        edge_in,
        edge_sem.at[0],
        edge_sem.at[1],
        device_id=(jnp.where(group_ends, lax.rem(stretch + 1, 16), stretch), jnp.where(group_ends, 0, grp + 1)),
        device_id_type=MESH,
    )

    @pl.when(jnp.logical_not(is_last))
    def _():
        edge_copy.start()

    def rest_of(p, g):
        block, rows = place(p, g)
        return signal.at[block, pl.ds(pl.multiple_of(rows.start + HEAD, HEAD), ROWS - HEAD)]

    def gated_copy(step):
        p, g = peer(step, 1)
        return pltpu.make_async_remote_copy(
            gated_buf.at[step],
            rest_of(piece, grp),
            gated_send.at[step],
            gated_recv.at[step],
            device_id=(plane * PIECES + p, g),
            device_id_type=MESH,
        )

    def head_copy(step):
        p, g = peer(step, 1)
        return pltpu.make_async_remote_copy(
            head_buf.at[step],
            heads.at[HALO_PIECES + piece, grp],
            head_send.at[step],
            head_recv.at[piece],
            device_id=(plane * PIECES + p, g),
            device_id_type=MESH,
        )

    own_rest = pltpu.make_async_copy(gated_buf.at[0], rest_of(piece, grp), gated_recv.at[0])
    own_rest.start()
    pl.semaphore_wait(plane_sem, PIECES - 1)

    def send_rest(step, carry):
        @pl.when(step >= AHEAD)
        def _():
            gate_rest(step)

        gated_copy(step).start()
        return carry

    lax.fori_loop(1, PEERS, send_rest, 0)

    def transform(source, block, target, rows):
        pair = jnp.concatenate([source[block], source[block + 1]], axis=1)
        bins = jnp.dot(forward[rows, :], jnp.concatenate([pair, pair], axis=0), preferred_element_type=F32)
        target[block, rows] = bins[:, :LANES]
        target[block + 1, rows] = bins[:, LANES:]

    def transform_blocks(source, target, first, pairs):
        def body(unit, carry):
            transform(source, first + 2 * lax.div(unit, 2), target, aligned(lax.rem(unit, 2), BLOCK))
            return carry

        lax.fori_loop(0, 2 * pairs, body, 0)

    @pl.when(is_first)
    def _():
        edge_in[...] = jnp.zeros_like(edge_in)

    @pl.when(jnp.logical_not(is_first))
    def _():
        edge_copy.wait_recv()

    for n in range(3):
        packed = edge_in[n].astype(F32)
        for r in range(2):
            for e in range(8):
                edge[n, r : r + 1, e * fold : (e + 1) * fold] = packed[r * 8 + e : r * 8 + e + 1]

    def send_head(step, carry):
        gate_first(step)
        head_copy(step).start()
        return carry

    lax.fori_loop(1, PEERS, send_head, 0)
    gate_first(0)
    own_head = pltpu.make_async_copy(head_buf.at[0], heads.at[HALO_PIECES + piece, grp], head_recv.at[piece])
    own_head.start()

    def shorten_q(block, carry):
        lanes = aligned(block, LANES)
        now = query_buf[:, lanes].astype(F32)
        q_buf[:, lanes] = shorten(now, edge[2, 0:1, lanes], edge[2, 1:2, lanes], 0, block).astype(BF16)
        return carry

    lax.fori_loop(0, PEERS, shorten_q, 0)
    ones[...] = jnp.ones_like(ones)
    q_rows = aligned(grp, ROWS)
    side_lanes = aligned(side, 2 * LANES)
    own_q = pltpu.make_async_copy(q_buf.at[:, aligned(grp, 512)], q_out.at[q_rows], own_sem.at[0])
    ones_copy = pltpu.make_async_copy(
        ones, q_out.at[aligned(1 - half, BLOCK), aligned(1 - side, 2 * LANES)], own_sem.at[2]
    )

    def q_near(step):
        other = half * 4 + lax.rem(row + step * around + 4, 4)
        return pltpu.make_async_remote_copy(
            q_buf.at[:, aligned(other, 512)],
            q_out.at[q_rows],
            q_send.at[step],
            q_recv.at[step],
            device_id=(stretch, other),
            device_id_type=MESH,
        )

    def q_far(step):
        other = (1 - half) * 4 + lax.rem(row + step * around + 4, 4)
        return pltpu.make_async_remote_copy(
            q_buf.at[:, aligned(other * 2 + side, 2 * LANES)],
            q_out.at[q_rows, side_lanes],
            q_send.at[4 + step],
            q_recv.at[4 + step],
            device_id=(stretch, other),
            device_id_type=MESH,
        )

    def q_aside(step):
        k = step % 2
        other, p = (1 - half) * 4 + lax.rem(row + step // 2 * around + 4, 4), 2 * (1 - side) + k
        return pltpu.make_async_remote_copy(
            q_buf.at[:, aligned(other * PIECES + p, LANES)],
            q_mid.at[core, aligned(row, ROWS)],
            q_mid_send.at[step],
            q_mid_recv.at[core],
            device_id=(plane * PIECES + p, other),
            device_id_type=MESH,
        )

    for step in range(8):
        q_aside(step).start()

    def send_q(turn):
        for step in FAR[turn]:
            q_far(step).start()
        for step in NEAR[turn]:
            q_near(step).start()

    own_q.start()
    ones_copy.start()

    loads[5].start()

    def halo_copy(p, g):
        block, rows = place(p, g)
        rest = pl.ds(pl.multiple_of(rows.start + HEAD, HEAD), ROWS - HEAD)
        return pltpu.make_async_remote_copy(
            signal.at[block, rest],
            signal.at[block - OWN, rest],
            halo_send.at[p, g],
            halo_recv.at[p],
            device_id=(lax.rem(stretch + PIECES, 16), grp),
            device_id_type=MESH,
        )

    def halo_head_copy(p):
        return pltpu.make_async_remote_copy(
            heads.at[HALO_PIECES + p],
            heads.at[p - 1],
            halo_head_send.at[p],
            halo_head_recv.at[p],
            device_id=(lax.rem(stretch + PIECES, 16), grp),
            device_id_type=MESH,
        )

    def receive(turn, carry):
        for p in (3, 2, 1, 0):
            step = 4 * turn + lax.rem(piece - p + 4, 4)
            _, g = peer(step, -1)
            rest = rest_of(p, g)
            pltpu.make_async_copy(rest, rest, gated_recv.at[step]).wait()
            if p >= PROMPT:

                @pl.when(has_after)
                def _():
                    halo_copy(p, g).start()

        return carry

    def settle(index, target):
        for c in range(GROUPS):
            signal[target + c // 4, (c % 4) * ROWS : (c % 4) * ROWS + HEAD] = heads[index, c]

    loads[3].wait()
    loads[4].wait()
    transform_blocks(filter_buf, filter_spectra, 0, HALO // 2)

    lax.fori_loop(0, GROUPS, receive, 0)
    for p in (3, 2, 1, 0):
        own_heads = heads.at[HALO_PIECES + p]
        pltpu.make_async_copy(own_heads, own_heads, head_recv.at[p]).wait()
        if p > 0:

            @pl.when(has_after)
            def _(p=p):
                halo_head_copy(p).start()
                if p < PROMPT:
                    for g in range(GROUPS):
                        halo_copy(p, g).start()

    send_q(0)
    for p in (3, 2, 1, 0):
        settle(HALO_PIECES + p, HALO + 2 * p)
    transform_blocks(signal, spectra, HALO, PIECES)

    gain = skip_gain[own_lanes].reshape(1, LANES)

    def wait_q_mid():
        for c in range(2):
            pltpu.make_async_copy(q_mid.at[c], q_mid.at[c], q_mid_recv.at[c]).wait()

    def convolve(p, first):
        def bins(tile, carry):
            real, imag = aligned(tile, 16), pl.ds(pl.multiple_of(BLOCK + tile * 16, 16), 16)
            window = []
            for b in range(HALO + 1):
                here, before = 2 * p + 1 + b, 2 * p + b
                window.append(
                    (
                        spectra[here, real] - spectra[before, imag],
                        spectra[here, imag] + spectra[before, real],
                    )
                )
            sums = [None, None]
            for i in range(HALO):
                fr, fi = filter_spectra[i, real], filter_spectra[i, imag]
                for o in range(2):
                    sr, si = window[HALO - 1 + o - i]
                    re, im = fr * sr - fi * si, fr * si + fi * sr
                    sums[o] = (re, im) if sums[o] is None else (sums[o][0] + re, sums[o][1] + im)
            for n, at_rows in ((0, real), (1, imag)):
                both = jnp.concatenate([sums[0][n], sums[1][n]], axis=1)
                high = both.astype(BF16)
                product[0, at_rows] = high
                product[1, at_rows] = (both - high.astype(F32)).astype(BF16)
            return carry

        lax.fori_loop(0, BLOCK // 16, bins, 0)
        high, low = product[0], product[1]
        back = jnp.dot(inverse[...], jnp.concatenate([high, low, high], axis=0), preferred_element_type=F32)
        for o in range(2):
            direct = gain * signal[HALO + 2 * p + o].astype(F32)
            total = back[:, o * LANES : (o + 1) * LANES] + direct
            here = jnp.logical_and(side != p // 2, half != o)

            @pl.when(here)
            def _():
                if first:
                    wait_q_mid()
                result[p, pl.ds(o * BLOCK, BLOCK)] = (total * q_mid[p % 2].astype(F32)).astype(BF16)

            @pl.when(jnp.logical_not(here))
            def _():
                result[p, pl.ds(o * BLOCK, BLOCK)] = total.astype(BF16)


    def r_copy(p):
        return pltpu.make_async_remote_copy(
            result.at[p],
            r_out.at[:, own_lanes],
            r_send.at[p],
            r_recv.at[piece],
            device_id=(plane * PIECES + p, grp),
            device_id_type=MESH,
        )

    own_r = pltpu.make_async_copy(result.at[piece], r_out.at[:, own_lanes], own_sem.at[1])

    def send_result(p):
        @pl.when(piece != p)
        def _():
            r_copy(p).start()

        @pl.when(piece == p)
        def _():
            own_r.start()

    def halo(p):
        @pl.when(has_before)
        def _():
            rests = signal.at[pl.ds(2 * p, 2), pl.ds(0, 4 * (ROWS - HEAD))]
            pltpu.make_async_copy(rests, rests, halo_recv.at[p + 1]).wait()
            pltpu.make_async_copy(heads.at[p], heads.at[p], halo_head_recv.at[p + 1]).wait()
            settle(p, 2 * p)

        transform_blocks(signal, spectra, 2 * p, 1)

    loads[5].wait()
    sides = set()
    for turn, (what, p) in enumerate(ORDER):
        if what == "halo":
            halo(p)
        else:
            convolve(p, p // 2 not in sides)
            sides.add(p // 2)
            send_result(p)
        send_q(1 + turn)

    own_q.wait()
    ones_copy.wait()
    own_r.wait()
    for p in range(PIECES):

        @pl.when(piece != p)
        def _(p=p):
            r_copy(p).wait_send()
            lanes = pl.ds(p * LANES, LANES)
            pltpu.make_async_copy(r_out.at[:, lanes], r_out.at[:, lanes], r_recv.at[p]).wait()

    for step in range(1, 4):
        q_near(step).wait()
    for step in range(4):
        q_far(step).wait()
    for step in range(8):
        q_aside(step).wait_send()

    @pl.when(jnp.logical_not(is_last))
    def _():
        edge_copy.wait_send()

    def sent(step, carry):
        gated_copy(step).wait_send()
        head_copy(step).wait_send()
        return carry

    lax.fori_loop(1, PEERS, sent, 0)

    @pl.when(has_after)
    def _():
        for p in range(1, PIECES):
            halo_head_copy(p).wait_send()

            def halo_sent(g, carry, p=p):
                halo_copy(p, g).wait_send()
                return carry

            lax.fori_loop(0, GROUPS, halo_sent, 0)


def multiply(q_ref, r_ref, out_ref):
    out_ref[...] = (q_ref[...].astype(F32) * r_ref[...].astype(F32)).astype(BF16)


def local(queries, keys, values, short_filter, long_filter, skip_gain):
    width = queries.shape[1]
    slice_width = width // GROUPS
    forward, inverse = tables()
    hbm, vmem = pl.BlockSpec(memory_space=pltpu.HBM), pl.BlockSpec(memory_space=pltpu.VMEM)
    anywhere = pl.BlockSpec(memory_space=pl.ANY)
    dma = pltpu.SemaphoreType.DMA
    q_slices, convolved = pl.pallas_call(
        kernel,
        out_shape=[jax.ShapeDtypeStruct((PIECE, slice_width), BF16)] * 2,
        in_specs=[hbm, hbm, hbm, hbm, hbm, vmem, hbm, hbm],
        out_specs=[anywhere, anywhere],
        scratch_shapes=[
            pltpu.VMEM((ROWS, width), BF16),
            pltpu.VMEM((ROWS, width), BF16),
            pltpu.VMEM((ROWS, width), BF16),
            pltpu.VMEM((3, 3, width), F32),
            pltpu.VMEM((HALO, BLOCK, LANES), BF16),
            pltpu.VMEM(forward.shape, BF16),
            pltpu.VMEM(inverse.shape, BF16),
            pltpu.VMEM((3, 16, 512), BF16),
            pltpu.VMEM((3, 16, 512), BF16),
            pltpu.VMEM((3, 8, width), F32),
            pltpu.VMEM((PEERS, ROWS - HEAD, LANES), BF16),
            pltpu.VMEM((PEERS, HEAD, LANES), BF16),
            pltpu.VMEM((HALO_PIECES + PIECES, GROUPS, HEAD, LANES), BF16),
            pltpu.VMEM((ROWS, width), BF16),
            pltpu.VMEM((2, BLOCK, LANES), BF16),
            pltpu.VMEM((BLOCK, 2 * LANES), BF16),
            pltpu.VMEM((HALO + OWN, BLOCK, LANES), BF16),
            pltpu.VMEM((HALO + OWN, 2 * BLOCK, LANES), F32),
            pltpu.VMEM((HALO, 2 * BLOCK, LANES), F32),
            pltpu.VMEM((2, 2 * BLOCK, 2 * LANES), BF16),
            pltpu.VMEM((PIECES, PIECE, LANES), BF16),
            dma((7,)),
            dma((2,)),
            pltpu.SemaphoreType.REGULAR,
            dma((PEERS,)),
            dma((PEERS,)),
            dma((PEERS,)),
            dma((PIECES,)),
            dma((PIECES, GROUPS)),
            dma((PIECES,)),
            dma((PIECES,)),
            dma((PIECES,)),
            dma((GROUPS,)),
            dma((GROUPS,)),
            dma((8,)),
            dma((2,)),
            dma((PIECES,)),
            dma((PIECES,)),
            dma((3,)),
        ],
        compiler_params=pltpu.CompilerParams(
            collective_id=0, has_side_effects=True, vmem_limit_bytes=VMEM_LIMIT
        ),
        cost_estimate=pl.CostEstimate(flops=9 * 10**9, bytes_accessed=16 * 2**20, transcendentals=0),
    )(
        queries,
        keys,
        values,
        short_filter,
        long_filter.reshape(HALO, BLOCK, slice_width),
        skip_gain,
        jnp.asarray(forward),
        jnp.asarray(inverse),
    )
    rows = PIECE // 2
    part = pl.BlockSpec((rows, slice_width), lambda i: (i, 0))
    return pl.pallas_call(
        multiply,
        out_shape=jax.ShapeDtypeStruct((PIECE, slice_width), BF16),
        grid=(2,),
        in_specs=[part, part],
        out_specs=part,
    )(q_slices, convolved)


def solution(mesh):
    return jax.shard_map(
        local,
        mesh=mesh,
        in_specs=(
            P(("stretch", "grp"), None),
            P(("stretch", "grp"), None),
            P(("stretch", "grp"), None),
            P(),
            P(None, "grp"),
            P("grp"),
        ),
        out_specs=P("stretch", "grp"),
        check_vma=False,
    )
```

```python
import jax
import jax.numpy as jnp
import ml_dtypes
import numpy as np
from jax import lax
from jax.experimental import pallas as pl
from jax.experimental.pallas import tpu as pltpu
from jax.sharding import PartitionSpec as P

MESH = pl.DeviceIdType.MESH
BLOCK = 512
LANES = 128
ROWS = 128
HEAD = 16
PIECES = 4
GROUPS = 8
PEERS = PIECES * GROUPS
PIECE = ROWS * GROUPS
TAPS = 3072
HALO = TAPS // BLOCK
OWN = PIECES * PIECE // BLOCK
HALO_PIECES = TAPS // PIECE
AHEAD = 8
PROMPT = 2
BF16, F32 = jnp.bfloat16, jnp.float32
FAR = ((0, 2), (1, 3), (), (), (), (), (), ())
NEAR = ((1, 3, 2), (), (), (), (), (), (), ())
ORDER = (
    ("piece", 3),
    ("halo", 2),
    ("halo", 1),
    ("piece", 1),
    ("piece", 2),
    ("halo", 0),
    ("piece", 0),
)
VMEM_LIMIT = 56 * 2**20


def tables():
    n, m = np.arange(BLOCK), np.arange(BLOCK)
    phase = ((4 * m[:, None] + 1) * n[None, :]) % (4 * BLOCK)
    angle = 2.0 * np.pi * phase / (4 * BLOCK)
    forward = np.concatenate([np.cos(angle), -np.sin(angle)], axis=0)

    def parts(table):
        high = table.astype(ml_dtypes.bfloat16)
        return high, (table - high.astype(np.float64)).astype(ml_dtypes.bfloat16)

    high, low = parts(forward)
    back_high, back_low = parts(forward.T / BLOCK)
    return np.concatenate([high, low], axis=1), np.concatenate([back_high, back_low], axis=1)


def kernel(
    queries,
    keys,
    values,
    short_filter,
    long_filter,
    skip_gain,
    forward_hbm,
    inverse_hbm,
    q_out,
    r_out,
    key_buf,
    value_buf,
    query_buf,
    short_buf,
    filter_buf,
    forward,
    inverse,
    edge_out,
    edge_in,
    edge,
    gated_buf,
    head_buf,
    heads,
    q_buf,
    q_mid,
    ones,
    signal,
    spectra,
    filter_spectra,
    product,
    result,
    load_sem,
    edge_sem,
    plane_sem,
    gated_send,
    gated_recv,
    head_send,
    head_recv,
    halo_send,
    halo_recv,
    halo_head_send,
    halo_head_recv,
    q_send,
    q_recv,
    q_mid_send,
    q_mid_recv,
    r_send,
    r_recv,
    own_sem,
):
    stretch, grp = lax.axis_index("stretch"), lax.axis_index("grp")
    plane, piece = lax.div(stretch, PIECES), lax.rem(stretch, PIECES)
    half, row = lax.div(grp, 4), lax.rem(grp, 4)
    side, core = lax.div(piece, 2), lax.rem(piece, 2)
    around = 1 - 2 * core
    has_before, has_after = plane > 0, plane < 3
    group_ends = grp == GROUPS - 1
    is_first = jnp.logical_and(stretch == 0, grp == 0)
    is_last = jnp.logical_and(stretch == 15, group_ends)

    def peer(step, sign):
        kp, ky, kx = lax.rem(step, 4), lax.div(step, 8), lax.rem(lax.div(step, 4), 2)
        p = lax.rem(piece + sign * kp + 4, 4)
        sender = core if sign > 0 else lax.rem(p, 2)
        y = lax.rem(row + sign * ky * (1 - 2 * sender) + 4, 4)
        h = lax.rem(half + kx, 2)
        return p, h * 4 + y

    def aligned(index, size):
        return pl.ds(pl.multiple_of(index * size, size), size)

    def place(p, g):
        return HALO + 2 * p + lax.div(g, 4), aligned(lax.rem(g, 4), ROWS)

    own_lanes = aligned(piece, LANES)
    loads = [
        pltpu.make_async_copy(keys, key_buf, load_sem.at[0]),
        pltpu.make_async_copy(values, value_buf, load_sem.at[1]),
        pltpu.make_async_copy(short_filter, short_buf, load_sem.at[2]),
        pltpu.make_async_copy(long_filter.at[:, :, own_lanes], filter_buf, load_sem.at[3]),
        pltpu.make_async_copy(forward_hbm, forward, load_sem.at[4]),
        pltpu.make_async_copy(inverse_hbm, inverse, load_sem.at[5]),
        pltpu.make_async_copy(queries, query_buf, load_sem.at[6]),
    ]
    for load in loads[:3] + loads[6:] + loads[3:5]:
        load.start()

    barrier = pltpu.get_barrier_semaphore()

    def tell(s, g):
        pl.semaphore_signal(barrier, inc=1, device_id=(s, g), device_id_type=MESH)

    for d in range(1, GROUPS):
        tell(stretch, lax.rem(grp + d, GROUPS))
    pieces = [plane * PIECES + lax.rem(piece + d, PIECES) for d in range(1, PIECES)]
    for s in pieces:
        tell(s, grp)

    @pl.when(has_before)
    def _():
        tell(stretch - PIECES, grp)

    @pl.when(jnp.logical_and(grp == 0, jnp.logical_not(is_first)))
    def _():
        tell(stretch - 1, GROUPS - 1)

    @pl.when(jnp.logical_not(has_before))
    def _():
        signal[:HALO] = jnp.zeros((HALO, BLOCK, LANES), BF16)

    for load in loads[:3]:
        load.wait()
    loads[6].wait()
    fold = 512
    row_at = lax.broadcasted_iota(jnp.int32, (16, fold), 0)
    for n, buf in enumerate((key_buf, value_buf, query_buf)):
        tail = buf[ROWS - 16 :, :].astype(F32)
        packed = jnp.zeros((16, fold), F32)
        for r in range(2):
            for e in range(8):
                part = tail[14 + r : 15 + r, e * fold : (e + 1) * fold]
                packed = jnp.where(row_at == r * 8 + e, part, packed)
        edge_out[n] = packed.astype(BF16)

    def shorten(now, two, one, position, block):
        at = lax.broadcasted_iota(jnp.int32, now.shape, 0)
        back1 = jnp.where(at == 0, one, pltpu.roll(now, 1, 0))
        back2 = jnp.where(at == 0, two, jnp.where(at == 1, one, pltpu.roll(now, 2, 0)))
        lanes = aligned(block, LANES)
        taps = [short_buf[tap, position : position + 1, lanes] for tap in range(3)]
        return taps[0] * now + taps[1] * back1 + taps[2] * back2

    def block_of(step):
        p, g = peer(step, 1)
        return g * PIECES + p

    def gate_first(step):
        block = block_of(step)
        lanes = aligned(block, LANES)
        factors = [
            shorten(buf[:HEAD, lanes].astype(F32), edge[n, 0:1, lanes], edge[n, 1:2, lanes], n + 1, block)
            for n, buf in enumerate((key_buf, value_buf))
        ]
        head_buf[step] = (factors[0] * factors[1]).astype(BF16)

    def gate_rest(step):
        block = block_of(step)
        lanes = aligned(block, LANES)
        factors = []
        for n, buf in enumerate((key_buf, value_buf)):
            now = buf[:, lanes].astype(F32)
            taps = [short_buf[tap, n + 1 : n + 2, lanes] for tap in range(3)]
            factors.append(taps[0] * now + taps[1] * pltpu.roll(now, 1, 0) + taps[2] * pltpu.roll(now, 2, 0))
        gated_buf[step] = (factors[0] * factors[1])[HEAD:].astype(BF16)

    def gate_ahead(step, carry):
        gate_rest(step)
        return carry

    lax.fori_loop(0, AHEAD, gate_ahead, 0)

    def count(flag):
        return flag.astype(jnp.int32)

    pl.semaphore_wait(
        barrier,
        GROUPS - 1 + PIECES - 1
        + count(has_after)
        + count(jnp.logical_and(group_ends, jnp.logical_not(is_last))),
    )
    for s in pieces:
        pl.semaphore_signal(plane_sem, inc=1, device_id=(s, grp), device_id_type=MESH)

    edge_copy = pltpu.make_async_remote_copy(
        edge_out,
        edge_in,
        edge_sem.at[0],
        edge_sem.at[1],
        device_id=(jnp.where(group_ends, lax.rem(stretch + 1, 16), stretch), jnp.where(group_ends, 0, grp + 1)),
        device_id_type=MESH,
    )

    @pl.when(jnp.logical_not(is_last))
    def _():
        edge_copy.start()

    def rest_of(p, g):
        block, rows = place(p, g)
        return signal.at[block, pl.ds(pl.multiple_of(rows.start + HEAD, HEAD), ROWS - HEAD)]

    def gated_copy(step):
        p, g = peer(step, 1)
        return pltpu.make_async_remote_copy(
            gated_buf.at[step],
            rest_of(piece, grp),
            gated_send.at[step],
            gated_recv.at[step],
            device_id=(plane * PIECES + p, g),
            device_id_type=MESH,
        )

    def head_copy(step):
        p, g = peer(step, 1)
        return pltpu.make_async_remote_copy(
            head_buf.at[step],
            heads.at[HALO_PIECES + piece, grp],
            head_send.at[step],
            head_recv.at[piece],
            device_id=(plane * PIECES + p, g),
            device_id_type=MESH,
        )

    own_rest = pltpu.make_async_copy(gated_buf.at[0], rest_of(piece, grp), gated_recv.at[0])
    own_rest.start()
    pl.semaphore_wait(plane_sem, PIECES - 1)

    def send_rest(step, carry):
        @pl.when(step >= AHEAD)
        def _():
            gate_rest(step)

        gated_copy(step).start()
        return carry

    lax.fori_loop(1, PEERS, send_rest, 0)

    def transform(source, block, target, rows):
        pair = jnp.concatenate([source[block], source[block + 1]], axis=1)
        bins = jnp.dot(forward[rows, :], jnp.concatenate([pair, pair], axis=0), preferred_element_type=F32)
        target[block, rows] = bins[:, :LANES]
        target[block + 1, rows] = bins[:, LANES:]

    def transform_blocks(source, target, first, pairs):
        def body(unit, carry):
            transform(source, first + 2 * lax.div(unit, 2), target, aligned(lax.rem(unit, 2), BLOCK))
            return carry

        lax.fori_loop(0, 2 * pairs, body, 0)

    @pl.when(is_first)
    def _():
        edge_in[...] = jnp.zeros_like(edge_in)

    @pl.when(jnp.logical_not(is_first))
    def _():
        edge_copy.wait_recv()

    for n in range(3):
        packed = edge_in[n].astype(F32)
        for r in range(2):
            for e in range(8):
                edge[n, r : r + 1, e * fold : (e + 1) * fold] = packed[r * 8 + e : r * 8 + e + 1]

    def send_head(step, carry):
        gate_first(step)
        head_copy(step).start()
        return carry

    lax.fori_loop(1, PEERS, send_head, 0)
    gate_first(0)
    own_head = pltpu.make_async_copy(head_buf.at[0], heads.at[HALO_PIECES + piece, grp], head_recv.at[piece])
    own_head.start()

    def shorten_q(block, carry):
        lanes = aligned(block, LANES)
        now = query_buf[:, lanes].astype(F32)
        q_buf[:, lanes] = shorten(now, edge[2, 0:1, lanes], edge[2, 1:2, lanes], 0, block).astype(BF16)
        return carry

    lax.fori_loop(0, PEERS, shorten_q, 0)
    ones[...] = jnp.ones_like(ones)
    q_rows = aligned(grp, ROWS)
    side_lanes = aligned(side, 2 * LANES)
    own_q = pltpu.make_async_copy(q_buf.at[:, aligned(grp, 512)], q_out.at[q_rows], own_sem.at[0])
    ones_copy = pltpu.make_async_copy(
        ones, q_out.at[aligned(1 - half, BLOCK), aligned(1 - side, 2 * LANES)], own_sem.at[2]
    )

    def q_near(step):
        other = half * 4 + lax.rem(row + step * around + 4, 4)
        return pltpu.make_async_remote_copy(
            q_buf.at[:, aligned(other, 512)],
            q_out.at[q_rows],
            q_send.at[step],
            q_recv.at[step],
            device_id=(stretch, other),
            device_id_type=MESH,
        )

    def q_far(step):
        other = (1 - half) * 4 + lax.rem(row + step * around + 4, 4)
        return pltpu.make_async_remote_copy(
            q_buf.at[:, aligned(other * 2 + side, 2 * LANES)],
            q_out.at[q_rows, side_lanes],
            q_send.at[4 + step],
            q_recv.at[4 + step],
            device_id=(stretch, other),
            device_id_type=MESH,
        )

    def q_aside(step):
        k = step % 2
        other, p = (1 - half) * 4 + lax.rem(row + step // 2 * around + 4, 4), 2 * (1 - side) + k
        return pltpu.make_async_remote_copy(
            q_buf.at[:, aligned(other * PIECES + p, LANES)],
            q_mid.at[core, aligned(row, ROWS)],
            q_mid_send.at[step],
            q_mid_recv.at[core],
            device_id=(plane * PIECES + p, other),
            device_id_type=MESH,
        )

    for step in range(8):
        q_aside(step).start()

    def send_q(turn):
        for step in FAR[turn]:
            q_far(step).start()
        for step in NEAR[turn]:
            q_near(step).start()

    own_q.start()
    ones_copy.start()

    loads[5].start()

    def halo_copy(p, g):
        block, rows = place(p, g)
        rest = pl.ds(pl.multiple_of(rows.start + HEAD, HEAD), ROWS - HEAD)
        return pltpu.make_async_remote_copy(
            signal.at[block, rest],
            signal.at[block - OWN, rest],
            halo_send.at[p, g],
            halo_recv.at[p],
            device_id=(lax.rem(stretch + PIECES, 16), grp),
            device_id_type=MESH,
        )

    def halo_head_copy(p):
        return pltpu.make_async_remote_copy(
            heads.at[HALO_PIECES + p],
            heads.at[p - 1],
            halo_head_send.at[p],
            halo_head_recv.at[p],
            device_id=(lax.rem(stretch + PIECES, 16), grp),
            device_id_type=MESH,
        )

    def receive(turn, carry):
        for p in (3, 2, 1, 0):
            step = 4 * turn + lax.rem(piece - p + 4, 4)
            _, g = peer(step, -1)
            rest = rest_of(p, g)
            pltpu.make_async_copy(rest, rest, gated_recv.at[step]).wait()
            if p >= PROMPT:

                @pl.when(has_after)
                def _():
                    halo_copy(p, g).start()

        return carry

    def settle(index, target):
        for c in range(GROUPS):
            signal[target + c // 4, (c % 4) * ROWS : (c % 4) * ROWS + HEAD] = heads[index, c]

    loads[3].wait()
    loads[4].wait()
    transform_blocks(filter_buf, filter_spectra, 0, HALO // 2)

    lax.fori_loop(0, GROUPS, receive, 0)
    for p in (3, 2, 1, 0):
        own_heads = heads.at[HALO_PIECES + p]
        pltpu.make_async_copy(own_heads, own_heads, head_recv.at[p]).wait()
        if p > 0:

            @pl.when(has_after)
            def _(p=p):
                halo_head_copy(p).start()
                if p < PROMPT:
                    for g in range(GROUPS):
                        halo_copy(p, g).start()

    send_q(0)
    for p in (3, 2, 1, 0):
        settle(HALO_PIECES + p, HALO + 2 * p)
    transform_blocks(signal, spectra, HALO, PIECES)

    gain = skip_gain[own_lanes].reshape(1, LANES)

    def wait_q_mid():
        for c in range(2):
            pltpu.make_async_copy(q_mid.at[c], q_mid.at[c], q_mid_recv.at[c]).wait()

    def convolve(p, first):
        def bins(tile, carry):
            real, imag = aligned(tile, 16), pl.ds(pl.multiple_of(BLOCK + tile * 16, 16), 16)
            window = []
            for b in range(HALO + 1):
                here, before = 2 * p + 1 + b, 2 * p + b
                window.append(
                    (
                        spectra[here, real] - spectra[before, imag],
                        spectra[here, imag] + spectra[before, real],
                    )
                )
            sums = [None, None]
            for i in range(HALO):
                fr, fi = filter_spectra[i, real], filter_spectra[i, imag]
                for o in range(2):
                    sr, si = window[HALO - 1 + o - i]
                    re, im = fr * sr - fi * si, fr * si + fi * sr
                    sums[o] = (re, im) if sums[o] is None else (sums[o][0] + re, sums[o][1] + im)
            for n, at_rows in ((0, real), (1, imag)):
                product[at_rows] = jnp.concatenate([sums[0][n], sums[1][n]], axis=1).astype(BF16)
            return carry

        lax.fori_loop(0, BLOCK // 16, bins, 0)
        twice = jnp.concatenate([product[...], product[...]], axis=0)
        back = jnp.dot(inverse[...], twice, preferred_element_type=F32)
        for o in range(2):
            direct = gain * signal[HALO + 2 * p + o].astype(F32)
            total = back[:, o * LANES : (o + 1) * LANES] + direct
            here = jnp.logical_and(side != p // 2, half != o)

            @pl.when(here)
            def _():
                if first:
                    wait_q_mid()
                result[p, pl.ds(o * BLOCK, BLOCK)] = (total * q_mid[p % 2].astype(F32)).astype(BF16)

            @pl.when(jnp.logical_not(here))
            def _():
                result[p, pl.ds(o * BLOCK, BLOCK)] = total.astype(BF16)


    def r_copy(p):
        return pltpu.make_async_remote_copy(
            result.at[p],
            r_out.at[:, own_lanes],
            r_send.at[p],
            r_recv.at[piece],
            device_id=(plane * PIECES + p, grp),
            device_id_type=MESH,
        )

    own_r = pltpu.make_async_copy(result.at[piece], r_out.at[:, own_lanes], own_sem.at[1])

    def send_result(p):
        @pl.when(piece != p)
        def _():
            r_copy(p).start()

        @pl.when(piece == p)
        def _():
            own_r.start()

    def halo(p):
        @pl.when(has_before)
        def _():
            rests = signal.at[pl.ds(2 * p, 2), pl.ds(0, 4 * (ROWS - HEAD))]
            pltpu.make_async_copy(rests, rests, halo_recv.at[p + 1]).wait()
            pltpu.make_async_copy(heads.at[p], heads.at[p], halo_head_recv.at[p + 1]).wait()
            settle(p, 2 * p)

        transform_blocks(signal, spectra, 2 * p, 1)

    loads[5].wait()
    sides = set()
    for turn, (what, p) in enumerate(ORDER):
        if what == "halo":
            halo(p)
        else:
            convolve(p, p // 2 not in sides)
            sides.add(p // 2)
            send_result(p)
        send_q(1 + turn)

    own_q.wait()
    ones_copy.wait()
    own_r.wait()
    for p in range(PIECES):

        @pl.when(piece != p)
        def _(p=p):
            r_copy(p).wait_send()
            lanes = pl.ds(p * LANES, LANES)
            pltpu.make_async_copy(r_out.at[:, lanes], r_out.at[:, lanes], r_recv.at[p]).wait()

    for step in range(1, 4):
        q_near(step).wait()
    for step in range(4):
        q_far(step).wait()
    for step in range(8):
        q_aside(step).wait_send()

    @pl.when(jnp.logical_not(is_last))
    def _():
        edge_copy.wait_send()

    def sent(step, carry):
        gated_copy(step).wait_send()
        head_copy(step).wait_send()
        return carry

    lax.fori_loop(1, PEERS, sent, 0)

    @pl.when(has_after)
    def _():
        for p in range(1, PIECES):
            halo_head_copy(p).wait_send()

            def halo_sent(g, carry, p=p):
                halo_copy(p, g).wait_send()
                return carry

            lax.fori_loop(0, GROUPS, halo_sent, 0)


def multiply(q_ref, r_ref, out_ref):
    out_ref[...] = (q_ref[...].astype(F32) * r_ref[...].astype(F32)).astype(BF16)


def local(queries, keys, values, short_filter, long_filter, skip_gain):
    width = queries.shape[1]
    slice_width = width // GROUPS
    forward, inverse = tables()
    hbm, vmem = pl.BlockSpec(memory_space=pltpu.HBM), pl.BlockSpec(memory_space=pltpu.VMEM)
    anywhere = pl.BlockSpec(memory_space=pl.ANY)
    dma = pltpu.SemaphoreType.DMA
    q_slices, convolved = pl.pallas_call(
        kernel,
        out_shape=[jax.ShapeDtypeStruct((PIECE, slice_width), BF16)] * 2,
        in_specs=[hbm, hbm, hbm, hbm, hbm, vmem, hbm, hbm],
        out_specs=[anywhere, anywhere],
        scratch_shapes=[
            pltpu.VMEM((ROWS, width), BF16),
            pltpu.VMEM((ROWS, width), BF16),
            pltpu.VMEM((ROWS, width), BF16),
            pltpu.VMEM((3, 3, width), F32),
            pltpu.VMEM((HALO, BLOCK, LANES), BF16),
            pltpu.VMEM(forward.shape, BF16),
            pltpu.VMEM(inverse.shape, BF16),
            pltpu.VMEM((3, 16, 512), BF16),
            pltpu.VMEM((3, 16, 512), BF16),
            pltpu.VMEM((3, 8, width), F32),
            pltpu.VMEM((PEERS, ROWS - HEAD, LANES), BF16),
            pltpu.VMEM((PEERS, HEAD, LANES), BF16),
            pltpu.VMEM((HALO_PIECES + PIECES, GROUPS, HEAD, LANES), BF16),
            pltpu.VMEM((ROWS, width), BF16),
            pltpu.VMEM((2, BLOCK, LANES), BF16),
            pltpu.VMEM((BLOCK, 2 * LANES), BF16),
            pltpu.VMEM((HALO + OWN, BLOCK, LANES), BF16),
            pltpu.VMEM((HALO + OWN, 2 * BLOCK, LANES), F32),
            pltpu.VMEM((HALO, 2 * BLOCK, LANES), F32),
            pltpu.VMEM((2 * BLOCK, 2 * LANES), BF16),
            pltpu.VMEM((PIECES, PIECE, LANES), BF16),
            dma((7,)),
            dma((2,)),
            pltpu.SemaphoreType.REGULAR,
            dma((PEERS,)),
            dma((PEERS,)),
            dma((PEERS,)),
            dma((PIECES,)),
            dma((PIECES, GROUPS)),
            dma((PIECES,)),
            dma((PIECES,)),
            dma((PIECES,)),
            dma((GROUPS,)),
            dma((GROUPS,)),
            dma((8,)),
            dma((2,)),
            dma((PIECES,)),
            dma((PIECES,)),
            dma((3,)),
        ],
        compiler_params=pltpu.CompilerParams(
            collective_id=0, has_side_effects=True, vmem_limit_bytes=VMEM_LIMIT
        ),
        cost_estimate=pl.CostEstimate(flops=9 * 10**9, bytes_accessed=16 * 2**20, transcendentals=0),
    )(
        queries,
        keys,
        values,
        short_filter,
        long_filter.reshape(HALO, BLOCK, slice_width),
        skip_gain,
        jnp.asarray(forward),
        jnp.asarray(inverse),
    )
    rows = PIECE // 2
    part = pl.BlockSpec((rows, slice_width), lambda i: (i, 0))
    return pl.pallas_call(
        multiply,
        out_shape=jax.ShapeDtypeStruct((PIECE, slice_width), BF16),
        grid=(2,),
        in_specs=[part, part],
        out_specs=part,
    )(q_slices, convolved)


def solution(mesh):
    return jax.shard_map(
        local,
        mesh=mesh,
        in_specs=(
            P(("stretch", "grp"), None),
            P(("stretch", "grp"), None),
            P(("stretch", "grp"), None),
            P(),
            P(None, "grp"),
            P("grp"),
        ),
        out_specs=P("stretch", "grp"),
        check_vma=False,
    )
```

```python
import jax
import jax.numpy as jnp
import ml_dtypes
import numpy as np
from jax import lax
from jax.experimental import pallas as pl
from jax.experimental.pallas import tpu as pltpu
from jax.sharding import PartitionSpec as P

MESH = pl.DeviceIdType.MESH
BLOCK = 512
LANES = 128
ROWS = 128
HEAD = 16
PIECES = 4
GROUPS = 8
PEERS = PIECES * GROUPS
PIECE = ROWS * GROUPS
TAPS = 3072
HALO = TAPS // BLOCK
OWN = PIECES * PIECE // BLOCK
HALO_PIECES = TAPS // PIECE
AHEAD = 8
PROMPT = 2
BF16, F32 = jnp.bfloat16, jnp.float32
FAR = ((0, 2), (1, 3), (), (), (), (), (), ())
NEAR = ((1, 3, 2), (), (), (), (), (), (), ())
ORDER = (
    ("piece", 3),
    ("halo", 2),
    ("halo", 1),
    ("piece", 1),
    ("piece", 2),
    ("halo", 0),
    ("piece", 0),
)
VMEM_LIMIT = 56 * 2**20


def tables():
    n, m = np.arange(BLOCK), np.arange(BLOCK)
    phase = ((4 * m[:, None] + 1) * n[None, :]) % (4 * BLOCK)
    angle = 2.0 * np.pi * phase / (4 * BLOCK)
    forward = np.concatenate([np.cos(angle), -np.sin(angle)], axis=0)

    def parts(table):
        high = table.astype(ml_dtypes.bfloat16)
        return high, (table - high.astype(np.float64)).astype(ml_dtypes.bfloat16)

    high, low = parts(forward)
    back_high, back_low = parts(forward.T / BLOCK)
    return np.concatenate([high, low], axis=1), np.concatenate([back_high, back_low], axis=1)


def kernel(
    queries,
    keys,
    values,
    short_filter,
    long_filter,
    skip_gain,
    forward_hbm,
    inverse_hbm,
    q_out,
    r_out,
    key_buf,
    value_buf,
    query_buf,
    short_buf,
    filter_buf,
    forward,
    inverse,
    edge_out,
    edge_in,
    edge,
    gated_buf,
    head_buf,
    heads,
    q_buf,
    q_mid,
    ones,
    signal,
    spectra,
    filter_spectra,
    product,
    result,
    load_sem,
    edge_sem,
    plane_sem,
    gated_send,
    gated_recv,
    head_send,
    head_recv,
    halo_send,
    halo_recv,
    halo_head_send,
    halo_head_recv,
    q_send,
    q_recv,
    q_mid_send,
    q_mid_recv,
    r_send,
    r_recv,
    own_sem,
):
    stretch, grp = lax.axis_index("stretch"), lax.axis_index("grp")
    plane, piece = lax.div(stretch, PIECES), lax.rem(stretch, PIECES)
    half, row = lax.div(grp, 4), lax.rem(grp, 4)
    side, core = lax.div(piece, 2), lax.rem(piece, 2)
    around = 1 - 2 * core
    has_before, has_after = plane > 0, plane < 3
    group_ends = grp == GROUPS - 1
    is_first = jnp.logical_and(stretch == 0, grp == 0)
    is_last = jnp.logical_and(stretch == 15, group_ends)

    def peer(step, sign):
        kp, ky, kx = lax.rem(step, 4), lax.div(step, 8), lax.rem(lax.div(step, 4), 2)
        p = lax.rem(piece + sign * kp + 4, 4)
        sender = core if sign > 0 else lax.rem(p, 2)
        y = lax.rem(row + sign * ky * (1 - 2 * sender) + 4, 4)
        h = lax.rem(half + kx, 2)
        return p, h * 4 + y

    def aligned(index, size):
        return pl.ds(pl.multiple_of(index * size, size), size)

    def place(p, g):
        return HALO + 2 * p + lax.div(g, 4), aligned(lax.rem(g, 4), ROWS)

    own_lanes = aligned(piece, LANES)
    loads = [
        pltpu.make_async_copy(keys, key_buf, load_sem.at[0]),
        pltpu.make_async_copy(values, value_buf, load_sem.at[1]),
        pltpu.make_async_copy(short_filter, short_buf, load_sem.at[2]),
        pltpu.make_async_copy(long_filter.at[:, :, own_lanes], filter_buf, load_sem.at[3]),
        pltpu.make_async_copy(forward_hbm, forward, load_sem.at[4]),
        pltpu.make_async_copy(inverse_hbm, inverse, load_sem.at[5]),
        pltpu.make_async_copy(queries, query_buf, load_sem.at[6]),
    ]
    for load in loads[:3] + loads[6:] + loads[3:5]:
        load.start()

    barrier = pltpu.get_barrier_semaphore()

    def tell(s, g):
        pl.semaphore_signal(barrier, inc=1, device_id=(s, g), device_id_type=MESH)

    for d in range(1, GROUPS):
        tell(stretch, lax.rem(grp + d, GROUPS))
    pieces = [plane * PIECES + lax.rem(piece + d, PIECES) for d in range(1, PIECES)]
    for s in pieces:
        tell(s, grp)

    @pl.when(has_before)
    def _():
        tell(stretch - PIECES, grp)

    @pl.when(jnp.logical_and(grp == 0, jnp.logical_not(is_first)))
    def _():
        tell(stretch - 1, GROUPS - 1)

    @pl.when(jnp.logical_not(has_before))
    def _():
        signal[:HALO] = jnp.zeros((HALO, BLOCK, LANES), BF16)

    for load in loads[:3]:
        load.wait()
    loads[6].wait()
    fold = 512
    row_at = lax.broadcasted_iota(jnp.int32, (16, fold), 0)
    for n, buf in enumerate((key_buf, value_buf, query_buf)):
        tail = buf[ROWS - 16 :, :].astype(F32)
        packed = jnp.zeros((16, fold), F32)
        for r in range(2):
            for e in range(8):
                part = tail[14 + r : 15 + r, e * fold : (e + 1) * fold]
                packed = jnp.where(row_at == r * 8 + e, part, packed)
        edge_out[n] = packed.astype(BF16)

    def shorten(now, two, one, position, block):
        at = lax.broadcasted_iota(jnp.int32, now.shape, 0)
        back1 = jnp.where(at == 0, one, pltpu.roll(now, 1, 0))
        back2 = jnp.where(at == 0, two, jnp.where(at == 1, one, pltpu.roll(now, 2, 0)))
        lanes = aligned(block, LANES)
        taps = [short_buf[tap, position : position + 1, lanes] for tap in range(3)]
        return taps[0] * now + taps[1] * back1 + taps[2] * back2

    def block_of(step):
        p, g = peer(step, 1)
        return g * PIECES + p

    def gate_first(step):
        block = block_of(step)
        lanes = aligned(block, LANES)
        factors = [
            shorten(buf[:HEAD, lanes].astype(F32), edge[n, 0:1, lanes], edge[n, 1:2, lanes], n + 1, block)
            for n, buf in enumerate((key_buf, value_buf))
        ]
        head_buf[step] = (factors[0] * factors[1]).astype(BF16)

    def gate_rest(step):
        block = block_of(step)
        lanes = aligned(block, LANES)
        factors = []
        for n, buf in enumerate((key_buf, value_buf)):
            now = buf[:, lanes].astype(F32)
            taps = [short_buf[tap, n + 1 : n + 2, lanes] for tap in range(3)]
            factors.append(taps[0] * now + taps[1] * pltpu.roll(now, 1, 0) + taps[2] * pltpu.roll(now, 2, 0))
        gated_buf[step] = (factors[0] * factors[1])[HEAD:].astype(BF16)

    def gate_ahead(step, carry):
        gate_rest(step)
        return carry

    lax.fori_loop(0, AHEAD, gate_ahead, 0)

    def count(flag):
        return flag.astype(jnp.int32)

    pl.semaphore_wait(
        barrier,
        GROUPS - 1 + PIECES - 1
        + count(has_after)
        + count(jnp.logical_and(group_ends, jnp.logical_not(is_last))),
    )
    for s in pieces:
        pl.semaphore_signal(plane_sem, inc=1, device_id=(s, grp), device_id_type=MESH)

    edge_copy = pltpu.make_async_remote_copy(
        edge_out,
        edge_in,
        edge_sem.at[0],
        edge_sem.at[1],
        device_id=(jnp.where(group_ends, lax.rem(stretch + 1, 16), stretch), jnp.where(group_ends, 0, grp + 1)),
        device_id_type=MESH,
    )

    @pl.when(jnp.logical_not(is_last))
    def _():
        edge_copy.start()

    def rest_of(p, g):
        block, rows = place(p, g)
        return signal.at[block, pl.ds(pl.multiple_of(rows.start + HEAD, HEAD), ROWS - HEAD)]

    def gated_copy(step):
        p, g = peer(step, 1)
        return pltpu.make_async_remote_copy(
            gated_buf.at[step],
            rest_of(piece, grp),
            gated_send.at[step],
            gated_recv.at[step],
            device_id=(plane * PIECES + p, g),
            device_id_type=MESH,
        )

    def head_copy(step):
        p, g = peer(step, 1)
        return pltpu.make_async_remote_copy(
            head_buf.at[step],
            heads.at[HALO_PIECES + piece, grp],
            head_send.at[step],
            head_recv.at[piece],
            device_id=(plane * PIECES + p, g),
            device_id_type=MESH,
        )

    own_rest = pltpu.make_async_copy(gated_buf.at[0], rest_of(piece, grp), gated_recv.at[0])
    own_rest.start()
    pl.semaphore_wait(plane_sem, PIECES - 1)

    def send_rest(step, carry):
        @pl.when(step >= AHEAD)
        def _():
            gate_rest(step)

        gated_copy(step).start()
        return carry

    lax.fori_loop(1, PEERS, send_rest, 0)

    def transform(source, block, target, rows):
        pair = jnp.concatenate([source[block], source[block + 1]], axis=1)
        bins = jnp.dot(forward[rows, :], jnp.concatenate([pair, pair], axis=0), preferred_element_type=F32)
        target[block, rows] = bins[:, :LANES]
        target[block + 1, rows] = bins[:, LANES:]

    def transform_blocks(source, target, first, pairs):
        def body(unit, carry):
            transform(source, first + 2 * lax.div(unit, 2), target, aligned(lax.rem(unit, 2), BLOCK))
            return carry

        lax.fori_loop(0, 2 * pairs, body, 0)

    @pl.when(is_first)
    def _():
        edge_in[...] = jnp.zeros_like(edge_in)

    @pl.when(jnp.logical_not(is_first))
    def _():
        edge_copy.wait_recv()

    for n in range(3):
        packed = edge_in[n].astype(F32)
        for r in range(2):
            for e in range(8):
                edge[n, r : r + 1, e * fold : (e + 1) * fold] = packed[r * 8 + e : r * 8 + e + 1]

    def send_head(step, carry):
        gate_first(step)
        head_copy(step).start()
        return carry

    lax.fori_loop(1, PEERS, send_head, 0)
    gate_first(0)
    own_head = pltpu.make_async_copy(head_buf.at[0], heads.at[HALO_PIECES + piece, grp], head_recv.at[piece])
    own_head.start()

    def shorten_q(block, carry):
        lanes = aligned(block, LANES)
        now = query_buf[:, lanes].astype(F32)
        q_buf[:, lanes] = shorten(now, edge[2, 0:1, lanes], edge[2, 1:2, lanes], 0, block).astype(BF16)
        return carry

    lax.fori_loop(0, PEERS, shorten_q, 0)
    ones[...] = jnp.ones_like(ones)
    q_rows = aligned(grp, ROWS)
    side_lanes = aligned(side, 2 * LANES)
    own_q = pltpu.make_async_copy(q_buf.at[:, aligned(grp, 512)], q_out.at[q_rows], own_sem.at[0])
    ones_copy = pltpu.make_async_copy(
        ones, q_out.at[aligned(1 - half, BLOCK), aligned(1 - side, 2 * LANES)], own_sem.at[2]
    )

    def q_near(step):
        other = half * 4 + lax.rem(row + step * around + 4, 4)
        return pltpu.make_async_remote_copy(
            q_buf.at[:, aligned(other, 512)],
            q_out.at[q_rows],
            q_send.at[step],
            q_recv.at[step],
            device_id=(stretch, other),
            device_id_type=MESH,
        )

    def q_far(step):
        other = (1 - half) * 4 + lax.rem(row + step * around + 4, 4)
        return pltpu.make_async_remote_copy(
            q_buf.at[:, aligned(other * 2 + side, 2 * LANES)],
            q_out.at[q_rows, side_lanes],
            q_send.at[4 + step],
            q_recv.at[4 + step],
            device_id=(stretch, other),
            device_id_type=MESH,
        )

    def q_aside(step):
        k = step % 2
        other, p = (1 - half) * 4 + lax.rem(row + step // 2 * around + 4, 4), 2 * (1 - side) + k
        return pltpu.make_async_remote_copy(
            q_buf.at[:, aligned(other * PIECES + p, LANES)],
            q_mid.at[core, aligned(row, ROWS)],
            q_mid_send.at[step],
            q_mid_recv.at[core],
            device_id=(plane * PIECES + p, other),
            device_id_type=MESH,
        )

    for step in range(8):
        q_aside(step).start()

    def send_q(turn):
        for step in FAR[turn]:
            q_far(step).start()
        for step in NEAR[turn]:
            q_near(step).start()

    own_q.start()
    ones_copy.start()

    loads[5].start()

    def halo_copy(p, g):
        block, rows = place(p, g)
        rest = pl.ds(pl.multiple_of(rows.start + HEAD, HEAD), ROWS - HEAD)
        return pltpu.make_async_remote_copy(
            signal.at[block, rest],
            signal.at[block - OWN, rest],
            halo_send.at[p, g],
            halo_recv.at[p],
            device_id=(lax.rem(stretch + PIECES, 16), grp),
            device_id_type=MESH,
        )

    def halo_head_copy(p):
        return pltpu.make_async_remote_copy(
            heads.at[HALO_PIECES + p],
            heads.at[p - 1],
            halo_head_send.at[p],
            halo_head_recv.at[p],
            device_id=(lax.rem(stretch + PIECES, 16), grp),
            device_id_type=MESH,
        )

    def receive(turn, carry):
        for p in (3, 2, 1, 0):
            step = 4 * turn + lax.rem(piece - p + 4, 4)
            _, g = peer(step, -1)
            rest = rest_of(p, g)
            pltpu.make_async_copy(rest, rest, gated_recv.at[step]).wait()
            if p >= PROMPT:

                @pl.when(has_after)
                def _():
                    halo_copy(p, g).start()

        return carry

    def settle(index, target):
        for c in range(GROUPS):
            signal[target + c // 4, (c % 4) * ROWS : (c % 4) * ROWS + HEAD] = heads[index, c]

    loads[3].wait()
    loads[4].wait()
    transform_blocks(filter_buf, filter_spectra, 0, HALO // 2)

    lax.fori_loop(0, GROUPS, receive, 0)
    for p in (3, 2, 1, 0):
        own_heads = heads.at[HALO_PIECES + p]
        pltpu.make_async_copy(own_heads, own_heads, head_recv.at[p]).wait()
        if p > 0:

            @pl.when(has_after)
            def _(p=p):
                halo_head_copy(p).start()
                if p < PROMPT:
                    for g in range(GROUPS):
                        halo_copy(p, g).start()

    send_q(0)
    for p in (3, 2, 1, 0):
        settle(HALO_PIECES + p, HALO + 2 * p)
    transform_blocks(signal, spectra, HALO, PIECES)

    gain = skip_gain[own_lanes].reshape(1, LANES)

    def wait_q_mid():
        for c in range(2):
            pltpu.make_async_copy(q_mid.at[c], q_mid.at[c], q_mid_recv.at[c]).wait()

    def convolve(p, first):
        def bins(tile, carry):
            real, imag = aligned(tile, 16), pl.ds(pl.multiple_of(BLOCK + tile * 16, 16), 16)
            window = []
            for b in range(HALO + 1):
                here, before = 2 * p + 1 + b, 2 * p + b
                window.append(
                    (
                        spectra[here, real] - spectra[before, imag],
                        spectra[here, imag] + spectra[before, real],
                    )
                )
            sums = [None, None]
            for i in range(HALO):
                fr, fi = filter_spectra[i, real], filter_spectra[i, imag]
                for o in range(2):
                    sr, si = window[HALO - 1 + o - i]
                    re, im = fr * sr - fi * si, fr * si + fi * sr
                    sums[o] = (re, im) if sums[o] is None else (sums[o][0] + re, sums[o][1] + im)
            for n, at_rows in ((0, real), (1, imag)):
                product[at_rows] = jnp.concatenate([sums[0][n], sums[1][n]], axis=1).astype(BF16)
            return carry

        lax.fori_loop(0, BLOCK // 16, bins, 0, unroll=2)
        twice = jnp.concatenate([product[...], product[...]], axis=0)
        back = jnp.dot(inverse[...], twice, preferred_element_type=F32)
        for o in range(2):
            direct = gain * signal[HALO + 2 * p + o].astype(F32)
            total = back[:, o * LANES : (o + 1) * LANES] + direct
            here = jnp.logical_and(side != p // 2, half != o)

            @pl.when(here)
            def _():
                if first:
                    wait_q_mid()
                result[p, pl.ds(o * BLOCK, BLOCK)] = (total * q_mid[p % 2].astype(F32)).astype(BF16)

            @pl.when(jnp.logical_not(here))
            def _():
                result[p, pl.ds(o * BLOCK, BLOCK)] = total.astype(BF16)


    def r_copy(p):
        return pltpu.make_async_remote_copy(
            result.at[p],
            r_out.at[:, own_lanes],
            r_send.at[p],
            r_recv.at[piece],
            device_id=(plane * PIECES + p, grp),
            device_id_type=MESH,
        )

    own_r = pltpu.make_async_copy(result.at[piece], r_out.at[:, own_lanes], own_sem.at[1])

    def send_result(p):
        @pl.when(piece != p)
        def _():
            r_copy(p).start()

        @pl.when(piece == p)
        def _():
            own_r.start()

    def halo(p):
        @pl.when(has_before)
        def _():
            rests = signal.at[pl.ds(2 * p, 2), pl.ds(0, 4 * (ROWS - HEAD))]
            pltpu.make_async_copy(rests, rests, halo_recv.at[p + 1]).wait()
            pltpu.make_async_copy(heads.at[p], heads.at[p], halo_head_recv.at[p + 1]).wait()
            settle(p, 2 * p)

        transform_blocks(signal, spectra, 2 * p, 1)

    loads[5].wait()
    sides = set()
    for turn, (what, p) in enumerate(ORDER):
        if what == "halo":
            halo(p)
        else:
            convolve(p, p // 2 not in sides)
            sides.add(p // 2)
            send_result(p)
        send_q(1 + turn)

    own_q.wait()
    ones_copy.wait()
    own_r.wait()
    for p in range(PIECES):

        @pl.when(piece != p)
        def _(p=p):
            r_copy(p).wait_send()
            lanes = pl.ds(p * LANES, LANES)
            pltpu.make_async_copy(r_out.at[:, lanes], r_out.at[:, lanes], r_recv.at[p]).wait()

    for step in range(1, 4):
        q_near(step).wait()
    for step in range(4):
        q_far(step).wait()
    for step in range(8):
        q_aside(step).wait_send()

    @pl.when(jnp.logical_not(is_last))
    def _():
        edge_copy.wait_send()

    def sent(step, carry):
        gated_copy(step).wait_send()
        head_copy(step).wait_send()
        return carry

    lax.fori_loop(1, PEERS, sent, 0)

    @pl.when(has_after)
    def _():
        for p in range(1, PIECES):
            halo_head_copy(p).wait_send()

            def halo_sent(g, carry, p=p):
                halo_copy(p, g).wait_send()
                return carry

            lax.fori_loop(0, GROUPS, halo_sent, 0)


def multiply(q_ref, r_ref, out_ref):
    out_ref[...] = (q_ref[...].astype(F32) * r_ref[...].astype(F32)).astype(BF16)


def local(queries, keys, values, short_filter, long_filter, skip_gain):
    width = queries.shape[1]
    slice_width = width // GROUPS
    forward, inverse = tables()
    hbm, vmem = pl.BlockSpec(memory_space=pltpu.HBM), pl.BlockSpec(memory_space=pltpu.VMEM)
    anywhere = pl.BlockSpec(memory_space=pl.ANY)
    dma = pltpu.SemaphoreType.DMA
    q_slices, convolved = pl.pallas_call(
        kernel,
        out_shape=[jax.ShapeDtypeStruct((PIECE, slice_width), BF16)] * 2,
        in_specs=[hbm, hbm, hbm, hbm, hbm, vmem, hbm, hbm],
        out_specs=[anywhere, anywhere],
        scratch_shapes=[
            pltpu.VMEM((ROWS, width), BF16),
            pltpu.VMEM((ROWS, width), BF16),
            pltpu.VMEM((ROWS, width), BF16),
            pltpu.VMEM((3, 3, width), F32),
            pltpu.VMEM((HALO, BLOCK, LANES), BF16),
            pltpu.VMEM(forward.shape, BF16),
            pltpu.VMEM(inverse.shape, BF16),
            pltpu.VMEM((3, 16, 512), BF16),
            pltpu.VMEM((3, 16, 512), BF16),
            pltpu.VMEM((3, 8, width), F32),
            pltpu.VMEM((PEERS, ROWS - HEAD, LANES), BF16),
            pltpu.VMEM((PEERS, HEAD, LANES), BF16),
            pltpu.VMEM((HALO_PIECES + PIECES, GROUPS, HEAD, LANES), BF16),
            pltpu.VMEM((ROWS, width), BF16),
            pltpu.VMEM((2, BLOCK, LANES), BF16),
            pltpu.VMEM((BLOCK, 2 * LANES), BF16),
            pltpu.VMEM((HALO + OWN, BLOCK, LANES), BF16),
            pltpu.VMEM((HALO + OWN, 2 * BLOCK, LANES), F32),
            pltpu.VMEM((HALO, 2 * BLOCK, LANES), F32),
            pltpu.VMEM((2 * BLOCK, 2 * LANES), BF16),
            pltpu.VMEM((PIECES, PIECE, LANES), BF16),
            dma((7,)),
            dma((2,)),
            pltpu.SemaphoreType.REGULAR,
            dma((PEERS,)),
            dma((PEERS,)),
            dma((PEERS,)),
            dma((PIECES,)),
            dma((PIECES, GROUPS)),
            dma((PIECES,)),
            dma((PIECES,)),
            dma((PIECES,)),
            dma((GROUPS,)),
            dma((GROUPS,)),
            dma((8,)),
            dma((2,)),
            dma((PIECES,)),
            dma((PIECES,)),
            dma((3,)),
        ],
        compiler_params=pltpu.CompilerParams(
            collective_id=0, has_side_effects=True, vmem_limit_bytes=VMEM_LIMIT
        ),
        cost_estimate=pl.CostEstimate(flops=9 * 10**9, bytes_accessed=16 * 2**20, transcendentals=0),
    )(
        queries,
        keys,
        values,
        short_filter,
        long_filter.reshape(HALO, BLOCK, slice_width),
        skip_gain,
        jnp.asarray(forward),
        jnp.asarray(inverse),
    )
    rows = PIECE // 2
    part = pl.BlockSpec((rows, slice_width), lambda i: (i, 0))
    return pl.pallas_call(
        multiply,
        out_shape=jax.ShapeDtypeStruct((PIECE, slice_width), BF16),
        grid=(2,),
        in_specs=[part, part],
        out_specs=part,
    )(q_slices, convolved)


def solution(mesh):
    return jax.shard_map(
        local,
        mesh=mesh,
        in_specs=(
            P(("stretch", "grp"), None),
            P(("stretch", "grp"), None),
            P(("stretch", "grp"), None),
            P(),
            P(None, "grp"),
            P("grp"),
        ),
        out_specs=P("stretch", "grp"),
        check_vma=False,
    )
```
